128 devices in a mesh: sub: 8 (over z_lo, x), rng: 16 (over z_hi, y, core).
Axes of the slice: x: 4, y: 4, z: 4 (z_hi: 2, z_lo: 2; z = z_hi * 2 + z_lo), core: 2. Of those that a mesh axis runs over, the one named last changes fastest.
Arguments:
- echoes: float32 [2048, 2, 12288], P(('sub', 'rng')), may hold values from -6 to 6
- filter_spectrum: float32 [2, 12288], replicated, may hold values from -3 to 3
- range_shifts: int32 [2048], P('sub'), may hold values from -16 to 16
- steering: bfloat16 [8, 2, 384, 256], P('sub'), may hold values from -0.25 to 0.25
- tap_offsets: int32 [8, 2, 384], P('sub'), may hold values from -3 to 3
- tap_weights: float32 [8, 2, 4, 384], P('sub'), may hold values from -2 to 2
- phase_rates: float32 [8, 2, 384], P('sub'), may hold values from -6 to 6
Outputs:
- tiles: float32 [3072, 2, 12288], P('sub', None, 'rng')
The draws below stay inside these ranges and needn't reach their ends.
All inputs are finite; a program needn't handle non-finite values.
Results may differ from the reference program's by a relative error of at most 0.0076.
Values may be sent and summed in bfloat16 or wider, within the bound.
A program may use at most 256 MiB of HBM per device.

```python
import jax
import jax.numpy as jnp
import numpy as np
from jax import lax

ANGLES = 384
TAPS = 4
HALO = 16
SAMPLES = 12288
PSUB = 256
SUBS = 8
PULSES = 2048
N_SUB = 8


def touch_ends(entries, key, least, high):
    dims = entries.shape
    spot = [jax.random.randint(jax.random.fold_in(key, axis), (), 0, dims[axis]) for axis in range(len(dims))]
    entries = entries.at[tuple(spot)].set(least)
    longest = dims.index(max(dims))
    spot[longest] = (spot[longest] + 1) % dims[longest]
    return entries.at[tuple(spot)].set(high)


def shard_levels(stream_key, shape, cuts, low, top_value):
    level, own = 1.0, jax.random.fold_in(stream_key, 6)
    for axis_at, shards_of in cuts:
        steps = jnp.exp(jax.random.uniform(jax.random.fold_in(own, axis_at), (shards_of,), jnp.float32, low / len(cuts), top_value / len(cuts)))
        level = level * jnp.repeat(steps, shape[axis_at] // shards_of).reshape([-1 if axis == axis_at else 1 for axis in range(len(shape))])
    return level


def gaussian(key, dims, deviation, most, cuts=(), kind=jnp.bfloat16):
    gain = shard_levels(key, dims, cuts, -0.22, 0.18) if cuts else 1.0
    array = jax.random.normal(key, dims, jnp.float32) * deviation * gain
    return jnp.minimum(jnp.maximum(array, -most), most).astype(kind)


def setup_inputs(seed: int = 0) -> dict:
    arg_keys = jax.random.split(jax.random.key(seed), 8)
    echoes = gaussian(arg_keys[0], (PULSES, 2, SAMPLES), 1.0, 6.0, ((0, 128),), jnp.float32)
    filter_spectrum = gaussian(arg_keys[1], (2, SAMPLES), 0.5, 3.0, (), jnp.float32)
    range_shifts = touch_ends(jax.random.randint(arg_keys[2], (PULSES,), 0 - HALO, HALO + 1), jax.random.fold_in(arg_keys[2], 1), 0 - HALO, HALO).astype(jnp.int32)
    steering = gaussian(arg_keys[3], (SUBS, 2, ANGLES, PSUB), (2 * PSUB) ** -0.5, 0.25, ((0, 8),))
    tap_offsets = touch_ends(jax.random.randint(arg_keys[4], (SUBS, 2, ANGLES), -3, 4), jax.random.fold_in(arg_keys[4], 1), -3, 3).astype(jnp.int32)
    tap_weights = gaussian(arg_keys[5], (SUBS, 2, TAPS, ANGLES), 0.35, 2.0, ((0, 8),), jnp.float32)
    phase_rates = jnp.clip(jax.random.uniform(arg_keys[6], (SUBS, 2, ANGLES), jnp.float32, -6.0, 6.0) * shard_levels(arg_keys[6], (SUBS, 2, ANGLES), ((0, 8),), -0.4, 0.0), -6.0, 6.0)
    return dict(echoes=echoes, filter_spectrum=filter_spectrum, range_shifts=range_shifts, steering=steering, tap_offsets=tap_offsets, tap_weights=tap_weights, phase_rates=phase_rates)


def interp_matrix(weights, offsets):
    angles = jnp.arange(ANGLES, dtype=jnp.int32)
    total = jnp.zeros((ANGLES, ANGLES), jnp.float32)
    for tap in range(TAPS):
        source = jnp.clip(angles + offsets + (tap - 1), 0, ANGLES - 1)
        total = total + weights[tap][:, None] * (angles[None, :] == source[:, None]).astype(jnp.float32)
    return total.astype(jnp.bfloat16)


def rotate(values, phase):
    cosine = jnp.cos(phase)
    sine = jnp.sin(phase)
    real = values[..., 0, :]
    imag = values[..., 1, :]
    return jnp.stack([real * cosine - imag * sine, real * sine + imag * cosine], axis=-2)


def one_group(inputs):
    echo, shifts, steer, spectrum = inputs
    signal = echo[:, 0] + 1j * echo[:, 1]
    filt = spectrum[0] + 1j * spectrum[1]
    out = jnp.fft.ifft(jnp.fft.fft(signal, axis=1) * filt[None, :], axis=1)
    compressed = jnp.stack([jnp.real(out), jnp.imag(out)], axis=1).astype(jnp.float32)
    padded = jnp.pad(compressed, ((0, 0), (0, 0), (HALO, HALO)))

    def cut(row, shift):
        return lax.dynamic_slice_in_dim(row, (HALO + shift).astype(jnp.int32), SAMPLES, 1)

    shifted = jax.vmap(cut)(padded, shifts).astype(jnp.bfloat16)
    mixed = jnp.dot(steer.reshape(2 * ANGLES, PSUB), shifted.reshape(PSUB, 2 * SAMPLES), preferred_element_type=jnp.float32)
    mixed = mixed.reshape(2, ANGLES, 2, SAMPLES)
    real = mixed[0, :, 0] - mixed[1, :, 1]
    imag = mixed[0, :, 1] + mixed[1, :, 0]
    return jnp.stack([real, imag], axis=1).astype(jnp.bfloat16)


def reference(echoes, filter_spectrum, range_shifts, steering, tap_offsets, tap_weights, phase_rates):
    spectra = jnp.broadcast_to(filter_spectrum, (N_SUB, 2, SAMPLES))
    image = lax.map(one_group, (echoes.reshape(N_SUB, PSUB, 2, SAMPLES), range_shifts.reshape(N_SUB, PSUB), steering, spectra))
    mats = jax.vmap(jax.vmap(interp_matrix))(tap_weights, tap_offsets)
    positions = jnp.arange(SAMPLES, dtype=jnp.float32) / SAMPLES
    levels = N_SUB.bit_length() - 1
    merged = None
    for level in range(levels):
        order = np.arange(N_SUB) ^ (1 << level)
        partner = image[order]
        scale = float(level + 1)
        own_part = jnp.einsum("iab,ibc->iac", mats[:, 0].astype(jnp.float32), image.reshape(N_SUB, ANGLES, 2 * SAMPLES).astype(jnp.float32)).reshape(N_SUB, ANGLES, 2, SAMPLES)
        far_part = jnp.einsum("iab,ibc->iac", mats[:, 1].astype(jnp.float32), partner.reshape(N_SUB, ANGLES, 2 * SAMPLES).astype(jnp.float32)).reshape(N_SUB, ANGLES, 2, SAMPLES)
        merged = rotate(own_part, phase_rates[:, 0][:, :, None] * scale * positions[None, None, :]) + rotate(far_part, phase_rates[:, 1][:, :, None] * scale * positions[None, None, :])
        image = merged.astype(jnp.bfloat16)
    return merged.reshape(N_SUB * ANGLES, 2, SAMPLES)
```

```python
import math

import jax
import jax.numpy as jnp
import ml_dtypes
import numpy as np
from jax import lax
from jax.experimental import pallas as pl
from jax.experimental.pallas import tpu as pltpu
from jax.sharding import PartitionSpec as P

RADIX_A = 96
RADIX_B = 128
ANGLES = 384
TAPS = 4
SAMPLES = 12288
SUBS = 8
RANKS = 16
PULSES = 16
PSUB = RANKS * PULSES
BLOCK = SAMPLES // RANKS
ROWS = BLOCK // RADIX_B
CHUNK = BLOCK // SUBS
LEVELS = 3
PARAMS = 16
MESH = pl.DeviceIdType.MESH
F32 = jnp.float32
BF16 = jnp.bfloat16


def halves(table):
    high = table.astype(np.float32).astype(ml_dtypes.bfloat16)
    low = (table - high.astype(np.float64)).astype(np.float32).astype(ml_dtypes.bfloat16)
    return np.stack([high, low])


def tables():
    a = np.arange(RADIX_A)
    b = np.arange(RADIX_B)
    wa = np.exp(-2j * np.pi / RADIX_A * (np.outer(a, a) % RADIX_A))
    wb = np.exp(-2j * np.pi / RADIX_B * (np.outer(b, b) % RADIX_B))
    order = 4 * (b % 32) + b // 32
    wb = wb[:, order]
    vb = np.conj(wb.T)
    va = np.conj(wa)
    left = lambda w: np.block([[w.real, -w.imag], [w.imag, w.real]])
    right = lambda w: np.block([[w.real, w.imag], [-w.imag, w.real]])
    turn = np.exp(-2j * np.pi / SAMPLES * np.outer(a, b))
    twiddle = np.stack([turn.real, turn.imag, turn.real / SAMPLES, -turn.imag / SAMPLES])
    return (
        halves(left(wa)),
        halves(right(wb)),
        halves(right(vb)),
        halves(left(va)),
        twiddle.astype(np.float32),
    )


def split(x):
    high = x.astype(BF16)
    return high, (x - high.astype(F32)).astype(BF16)


def dot(left, right):
    return jnp.dot(left, right, preferred_element_type=F32)


def left_product(table, x):
    high, low = split(x)
    return dot(table[0], high) + dot(table[0], low) + dot(table[1], high)


def right_product(x, table):
    high, low = split(x)
    return dot(high, table[0]) + dot(low, table[0]) + dot(high, table[1])


def times(ar, ai, br, bi):
    return ar * br - ai * bi, ar * bi + ai * br


def compress_kernel(shift_ref, x_ref, f_ref, wa, wb, vb, va, tw, out_ref, filt, rows):
    first = lax.axis_index("rng") * PULSES
    lane32 = lax.broadcasted_iota(jnp.int32, (32, RADIX_B), 1)
    for c in range(2):
        f0, f1, f2 = (f_ref[pl.ds(2 * e + c, 32, stride=6), :] for e in range(3))
        parts = [
            f0,
            jnp.where(lane32 < 32, pltpu.roll(f0, 32, 1), pltpu.roll(f1, 32, 1)),
            jnp.where(lane32 < 64, pltpu.roll(f1, 64, 1), pltpu.roll(f2, 64, 1)),
            pltpu.roll(f2, 96, 1),
        ]
        filt[c] = jnp.concatenate(parts, axis=0).T[:RADIX_A]
    lane = lax.broadcasted_iota(jnp.int32, (RADIX_A, RADIX_B), 1)
    row = lax.broadcasted_iota(jnp.int32, (RADIX_A, RADIX_B), 0)

    def pair(i, carry):
        start = i * 4 * RADIX_A
        signal = jnp.concatenate(
            [
                jnp.concatenate(
                    [x_ref[pl.ds(start + q * 2 * RADIX_A + c, RADIX_A, stride=2), :] for c in range(2)],
                    axis=0,
                )
                for q in range(2)
            ],
            axis=1,
        )
        section = left_product(wa, signal)
        turned = []
        for q in range(2):
            cols = slice(q * RADIX_B, (q + 1) * RADIX_B)
            zr, zi = times(section[:RADIX_A, cols], section[RADIX_A:, cols], tw[0], tw[1])
            turned.append(jnp.concatenate([zr, zi], axis=1))
        spectrum = right_product(jnp.concatenate(turned, axis=0), wb)
        filtered = []
        for q in range(2):
            part = spectrum[q * RADIX_A : (q + 1) * RADIX_A]
            zr, zi = times(part[:, :RADIX_B], part[:, RADIX_B:], filt[0], filt[1])
            filtered.append(jnp.concatenate([zr, zi], axis=1))
        section = right_product(jnp.concatenate(filtered, axis=0), vb)
        turned = []
        for q in range(2):
            part = section[q * RADIX_A : (q + 1) * RADIX_A]
            zr, zi = times(part[:, :RADIX_B], part[:, RADIX_B:], tw[2], tw[3])
            turned.append(jnp.concatenate([zr, zi], axis=0))
        result = left_product(va, jnp.concatenate(turned, axis=1))
        for q in range(2):
            p = 2 * i + q
            shift = shift_ref[first + p]
            step = jnp.where(shift > 0, 1, -1)
            source = lane + shift
            inside = jnp.logical_and(source >= 0, source < RADIX_B)
            next_row = row + step
            present = jnp.logical_and(next_row >= 0, next_row < RADIX_A)
            for c in range(2):
                values = result[c * RADIX_A : (c + 1) * RADIX_A, q * RADIX_B : (q + 1) * RADIX_B]
                turned_lanes = pltpu.roll(values, lax.rem(RADIX_B - shift, RADIX_B), 1)
                beside = pltpu.roll(turned_lanes, lax.rem(RADIX_A - step, RADIX_A), 0)
                moved = jnp.where(inside, turned_lanes, jnp.where(present, beside, 0.0))
                rows[pl.ds(c * RADIX_A * PULSES + p, RADIX_A, stride=PULSES), :] = moved
        return carry

    lax.fori_loop(0, PULSES // 2, pair, 0)

    def pack(j, carry):
        for c in range(2):
            start = pl.multiple_of((c * RADIX_A + j * ROWS) * PULSES, ROWS * PULSES)
            block = rows[pl.ds(start, ROWS * PULSES), :].astype(BF16)
            out_ref[j, c] = block.reshape(ROWS, PULSES, RADIX_B)
        return carry

    lax.fori_loop(0, RANKS, pack, 0)


def partner_of(group, level):
    bit = 1 << level
    return group + bit - 2 * bit * lax.rem(group // bit, 2)


def merge_kernel(
    pulses_ref, steer_ref, off_ref, weight_ref, rate_ref, out_ref,
    held, params, left, steer, band, phase, sent, image, done,
    pulse_send, pulse_recv, param_send, param_recv, image_send, image_recv, tile_send, tile_recv, local_sem,
):
    sub = lax.axis_index("sub")
    rng = lax.axis_index("rng")
    barrier = pltpu.get_barrier_semaphore()
    for k in range(1, RANKS):
        pl.semaphore_signal(barrier, inc=1, device_id={"rng": lax.rem(rng + k, RANKS)}, device_id_type=MESH)
    for k in range(1, SUBS):
        pl.semaphore_signal(barrier, inc=1, device_id={"sub": lax.rem(sub + k, SUBS)}, device_id_type=MESH)
    pl.semaphore_wait(barrier, RANKS + SUBS - 2)

    def pulse_copy(slot_src, slot_dst, peer, dst_sem):
        return pltpu.make_async_remote_copy(
            src_ref=pulses_ref.at[slot_src], dst_ref=held.at[slot_dst], send_sem=pulse_send.at[slot_src],
            recv_sem=pulse_recv.at[dst_sem], device_id={"rng": peer}, device_id_type=MESH,
        )

    for k in range(1, RANKS):
        peer = lax.rem(rng + k, RANKS)
        pulse_copy(peer, rng, peer, rng).start()
    own_pulses = pltpu.make_async_copy(pulses_ref.at[rng], held.at[rng], local_sem.at[0])
    own_pulses.start()

    for h in range(2):
        params[sub, 8 * h : 8 * h + 1, :] = off_ref[h : h + 1, :].astype(F32)
        params[sub, 8 * h + 1 : 8 * h + 5, :] = weight_ref[TAPS * h : TAPS * (h + 1), :]
        params[sub, 8 * h + 5 : 8 * h + 6, :] = rate_ref[h : h + 1, :]
        params[sub, 8 * h + 6 : 8 * h + 8, :] = jnp.zeros((2, ANGLES), F32)

    def param_copy(slot, peer):
        return pltpu.make_async_remote_copy(
            src_ref=params.at[slot], dst_ref=params.at[slot], send_sem=param_send.at[peer],
            recv_sem=param_recv.at[slot], device_id={"sub": peer}, device_id_type=MESH,
        )

    for k in range(1, SUBS):
        param_copy(sub, lax.rem(sub + k, SUBS)).start()

    real = steer_ref[0].astype(F32)
    imag = steer_ref[1].astype(F32)
    steer[:PSUB, :ANGLES] = real.T.astype(BF16)
    steer[:PSUB, ANGLES:] = imag.T.astype(BF16)
    steer[PSUB:, :ANGLES] = (-imag).T.astype(BF16)
    steer[PSUB:, ANGLES:] = real.T.astype(BF16)

    for k in range(1, SUBS):
        peer = lax.rem(sub + k, SUBS)
        param_copy(peer, peer).wait_recv()

    angle = lax.broadcasted_iota(jnp.int32, (1, ANGLES), 1).astype(F32)
    across = lax.broadcasted_iota(jnp.int32, (RADIX_B, ANGLES), 0).astype(F32)
    lane8 = lax.broadcasted_iota(jnp.int32, (8, ANGLES), 0)
    base = rng * BLOCK + sub * CHUNK

    def prepare(group, carry):
        for h in range(2):
            offset = params[group, 8 * h : 8 * h + 1, :]
            sources = [jnp.clip(angle + offset + float(t - 1), 0.0, ANGLES - 1.0) for t in range(TAPS)]
            weights = [params[group, 8 * h + 1 + t : 8 * h + 2 + t, :] for t in range(TAPS)]
            for part in range(ANGLES // RADIX_B):
                here = across + float(part * RADIX_B)
                total = jnp.zeros((RADIX_B, ANGLES), F32)
                for t in range(TAPS):
                    total = total + jnp.where(here == sources[t], weights[t], 0.0)
                band[2 * group + h, part * RADIX_B : (part + 1) * RADIX_B, :] = total.astype(BF16)
            rate = params[group, 8 * h + 5 : 8 * h + 6, :]
            at = rate * ((base + lane8).astype(F32) / SAMPLES)
            pr, pi = jnp.cos(at), jnp.sin(at)
            by = jnp.broadcast_to(rate * (8.0 / SAMPLES), (8, ANGLES))
            sr, si = jnp.cos(by), jnp.sin(by)
            for t in range(CHUNK // 8):
                rows = slice(8 * t, 8 * t + 8)
                qr, qi = pr, pi
                for level in range(LEVELS):
                    phase[level, 2 * group + h, 0, rows, :] = qr
                    phase[level, 2 * group + h, 1, rows, :] = qi
                    if level < LEVELS - 1:
                        qr, qi = times(qr, qi, pr, pi)
                pr, pi = times(pr, pi, sr, si)
        return carry

    lax.fori_loop(0, SUBS, prepare, 0)

    own_pulses.wait()
    for k in range(1, RANKS):
        peer = lax.rem(rng + k, RANKS)
        pulse_copy(peer, peer, peer, peer).wait_recv()

    for row in range(ROWS):
        for c in range(2):
            block = held[:, c, row].reshape(PSUB, RADIX_B)
            left[row * RADIX_B : (row + 1) * RADIX_B, c * PSUB : (c + 1) * PSUB] = block.T

    def image_copy(slot_src, slot_dst, peer):
        return pltpu.make_async_remote_copy(
            src_ref=sent.at[slot_src], dst_ref=image.at[0, slot_dst], send_sem=image_send.at[slot_src],
            recv_sem=image_recv.at[slot_dst], device_id={"sub": peer}, device_id_type=MESH,
        )

    for k in range(1, SUBS + 1):
        peer = lax.rem(sub + k, SUBS)
        bins = pl.ds(pl.multiple_of(peer * CHUNK, CHUNK), CHUNK)
        part = dot(left[bins, :], steer[...]).astype(BF16)
        for c in range(2):
            values = part[:, c * ANGLES : (c + 1) * ANGLES]
            if k < SUBS:
                sent[peer, c] = values
            else:
                image[0, sub, c] = values
        if k < SUBS:
            image_copy(peer, sub, peer).start()
    for k in range(1, SUBS):
        peer = lax.rem(sub + k, SUBS)
        image_copy(peer, peer, peer).wait_recv()

    def merge(level, group):
        now = level % 2
        far_group = partner_of(group, level)
        own = dot(image[now, group].reshape(2 * CHUNK, ANGLES), band[2 * group])
        far = dot(image[now, far_group].reshape(2 * CHUNK, ANGLES), band[2 * group + 1])
        ar, ai = times(own[:CHUNK], own[CHUNK:], phase[level, 2 * group, 0], phase[level, 2 * group, 1])
        br, bi = times(far[:CHUNK], far[CHUNK:], phase[level, 2 * group + 1, 0], phase[level, 2 * group + 1, 1])
        return ((ar + br).astype(BF16), (ai + bi).astype(BF16))

    for level in range(LEVELS - 1):

        def step(group, carry):
            real, imag = merge(level, group)
            image[(level + 1) % 2, group, 0] = real
            image[(level + 1) % 2, group, 1] = imag
            return carry

        lax.fori_loop(0, SUBS, step, 0)

    def tile_copy(slot_src, slot_dst, peer):
        return pltpu.make_async_remote_copy(
            src_ref=done.at[slot_src], dst_ref=out_ref.at[slot_dst], send_sem=tile_send.at[slot_src],
            recv_sem=tile_recv.at[slot_dst], device_id={"sub": peer}, device_id_type=MESH,
        )

    for k in range(1, SUBS + 1):
        peer = lax.rem(sub + k, SUBS)
        real, imag = merge(LEVELS - 1, peer)
        done[peer, 0] = real
        done[peer, 1] = imag
        if k < SUBS:
            tile_copy(peer, sub, peer).start()
    own_tile = pltpu.make_async_copy(done.at[sub], out_ref.at[sub], local_sem.at[1])
    own_tile.start()
    own_tile.wait()
    for k in range(1, SUBS):
        peer = lax.rem(sub + k, SUBS)
        tile_copy(peer, peer, peer).wait_recv()
    for k in range(1, RANKS):
        peer = lax.rem(rng + k, RANKS)
        pulse_copy(peer, rng, peer, rng).wait_send()
    for k in range(1, SUBS):
        peer = lax.rem(sub + k, SUBS)
        param_copy(sub, peer).wait_send()
        image_copy(peer, sub, peer).wait_send()
        tile_copy(peer, sub, peer).wait_send()


def tile_kernel(x_ref, out_ref):
    for c in range(2):
        image = x_ref[:, c].reshape(BLOCK, ANGLES)
        for row in range(ROWS):
            for part in range(ANGLES // RADIX_B):
                bins = slice(row * RADIX_B, (row + 1) * RADIX_B)
                angles = slice(part * RADIX_B, (part + 1) * RADIX_B)
                out_ref[angles, c, bins] = image[bins, angles].astype(F32).T


def vmem():
    return pl.BlockSpec(memory_space=pltpu.VMEM)


def local(echoes, filter_spectrum, range_shifts, steering, tap_offsets, tap_weights, phase_rates):
    rows = echoes.reshape(PULSES, 2, RADIX_A, RADIX_B).transpose(0, 2, 1, 3).reshape(-1, RADIX_B)
    filt = filter_spectrum.reshape(2, RADIX_A, RADIX_B).transpose(1, 0, 2).reshape(-1, RADIX_B)
    consts = [jnp.asarray(t) for t in tables()]
    pulses = pl.pallas_call(
        compress_kernel,
        out_shape=jax.ShapeDtypeStruct((RANKS, 2, ROWS, PULSES, RADIX_B), BF16),
        in_specs=[pl.BlockSpec(memory_space=pltpu.SMEM)] + [vmem()] * 7,
        out_specs=vmem(),
        scratch_shapes=[
            pltpu.VMEM((2, RADIX_A, RADIX_B), F32),
            pltpu.VMEM((2 * RADIX_A * PULSES, RADIX_B), F32),
        ],
        compiler_params=pltpu.CompilerParams(vmem_limit_bytes=32 << 20),
        name="compress",
    )(range_shifts, rows, filt, *consts)
    anywhere = pl.BlockSpec(memory_space=pl.ANY)
    dma = pltpu.SemaphoreType.DMA
    merged = pl.pallas_call(
        merge_kernel,
        out_shape=jax.ShapeDtypeStruct((SUBS, 2, CHUNK, ANGLES), BF16),
        in_specs=[anywhere] + [vmem()] * 4,
        out_specs=anywhere,
        scratch_shapes=[
            pltpu.VMEM((RANKS, 2, ROWS, PULSES, RADIX_B), BF16),
            pltpu.VMEM((SUBS, PARAMS, ANGLES), F32),
            pltpu.VMEM((BLOCK, 2 * PSUB), BF16),
            pltpu.VMEM((2 * PSUB, 2 * ANGLES), BF16),
            pltpu.VMEM((2 * SUBS, ANGLES, ANGLES), BF16),
            pltpu.VMEM((LEVELS, 2 * SUBS, 2, CHUNK, ANGLES), F32),
            pltpu.VMEM((SUBS, 2, CHUNK, ANGLES), BF16),
            pltpu.VMEM((2, SUBS, 2, CHUNK, ANGLES), BF16),
            pltpu.VMEM((SUBS, 2, CHUNK, ANGLES), BF16),
            dma((RANKS,)), dma((RANKS,)), dma((SUBS,)), dma((SUBS,)), dma((SUBS,)), dma((SUBS,)),
            dma((SUBS,)), dma((SUBS,)), dma((2,)),
        ],
        compiler_params=pltpu.CompilerParams(
            collective_id=0, has_side_effects=True, vmem_limit_bytes=56 << 20
        ),
        name="merge",
    )(
        pulses,
        steering.reshape(2, ANGLES, PSUB),
        tap_offsets.reshape(2, ANGLES),
        tap_weights.reshape(2 * TAPS, ANGLES),
        phase_rates.reshape(2, ANGLES),
    )
    return pl.pallas_call(
        tile_kernel,
        out_shape=jax.ShapeDtypeStruct((ANGLES, 2, BLOCK), F32),
        in_specs=[vmem()],
        out_specs=vmem(),
        compiler_params=pltpu.CompilerParams(vmem_limit_bytes=32 << 20),
        name="tile",
    )(merged)


def solution(mesh):
    placed = (
        P(("sub", "rng"), None, None),
        P(),
        P("sub"),
        P("sub", None, None, None),
        P("sub", None, None),
        P("sub", None, None, None),
        P("sub", None, None),
    )
    return jax.shard_map(
        local, mesh=mesh, in_specs=placed, out_specs=P("sub", None, "rng"), check_vma=False
    )
```

```python
import math

import jax
import jax.numpy as jnp
import ml_dtypes
import numpy as np
from jax import lax
from jax.experimental import pallas as pl
from jax.experimental.pallas import tpu as pltpu
from jax.sharding import PartitionSpec as P

RADIX_A = 96
RADIX_B = 128
ANGLES = 384
TAPS = 4
SAMPLES = 12288
SUBS = 8
RANKS = 16
PULSES = 16
PSUB = RANKS * PULSES
BLOCK = SAMPLES // RANKS
ROWS = BLOCK // RADIX_B
STAGES = 2
STAGE_ROWS = ROWS // STAGES
STAGE_BINS = BLOCK // STAGES
PIECE = STAGE_BINS // SUBS
PAIRS = 2
STEPS = PULSES // (2 * PAIRS)
HALO = 16
LEVELS = 3
PARAMS = 16
MESH = pl.DeviceIdType.MESH
F32 = jnp.float32
BF16 = jnp.bfloat16


def halves(table, axis):
    high = table.astype(np.float32).astype(ml_dtypes.bfloat16)
    low = (table - high.astype(np.float64)).astype(np.float32).astype(ml_dtypes.bfloat16)
    return np.concatenate([high, high, low], axis=axis)


def tables():
    a = np.arange(RADIX_A)
    b = np.arange(RADIX_B)
    wa = np.exp(-2j * np.pi / RADIX_A * (np.outer(a, a) % RADIX_A))
    wb = np.exp(-2j * np.pi / RADIX_B * (np.outer(b, b) % RADIX_B))
    order = 4 * (b % 32) + b // 32
    wb = wb[:, order]
    vb = np.conj(wb.T)
    va = np.conj(wa)
    left = lambda w: halves(np.block([[w.real, -w.imag], [w.imag, w.real]]), 1)
    right = lambda w: halves(np.block([[w.real, w.imag], [-w.imag, w.real]]), 0)
    turn = np.exp(-2j * np.pi / SAMPLES * np.outer(a, b))
    shifts = np.arange(-HALO, HALO + 1)
    back = np.exp(2j * np.pi / SAMPLES * a[None, :, None] * (b[None, None, :] + shifts[:, None, None])) / SAMPLES
    columns = np.exp(2j * np.pi / RADIX_B * (np.outer(shifts, order) % RADIX_B))
    lanes = np.zeros((2 * HALO + 1, 8, RADIX_B))
    lanes[:, 0], lanes[:, 1] = columns.real, columns.imag
    return (
        left(wa),
        right(wb),
        right(vb),
        left(va),
        np.stack([turn.real, turn.imag]).astype(np.float32),
        np.stack([back.real, back.imag], axis=1).astype(np.float32),
        lanes.astype(np.float32),
    )


def split(x):
    high = x.astype(BF16)
    return high, (x - high.astype(F32)).astype(BF16)


def dot(left, right):
    return jnp.dot(left, right, preferred_element_type=F32)


def left_product(table, x):
    high, low = split(x)
    return dot(table, jnp.concatenate([high, low, high], axis=0))


def right_product(x, table):
    high, low = split(x)
    return dot(jnp.concatenate([high, low, high], axis=1), table)


def times(ar, ai, br, bi):
    return ar * br - ai * bi, ar * bi + ai * br


def load_filter(f_ref, filt):
    lane32 = lax.broadcasted_iota(jnp.int32, (32, RADIX_B), 1)
    for c in range(2):
        f0, f1, f2 = (f_ref[pl.ds(2 * e + c, 32, stride=6), :] for e in range(3))
        parts = [
            f0,
            jnp.where(lane32 < 32, pltpu.roll(f0, 32, 1), pltpu.roll(f1, 32, 1)),
            jnp.where(lane32 < 64, pltpu.roll(f1, 64, 1), pltpu.roll(f2, 64, 1)),
            pltpu.roll(f2, 96, 1),
        ]
        filt[c] = jnp.concatenate(parts, axis=0).T[:RADIX_A]


def compress(i, first, shift_ref, x_ref, filt, wa, wb, vb, va, tw, back, lanes, rows):
    pairs = range(PAIRS)
    pulse = [[(i * PAIRS + j) * 2 + q for q in range(2)] for j in pairs]
    shift = [[shift_ref[first + p] for p in two] for two in pulse]
    results = []
    for j in pairs:
        signal = []
        for q in range(2):
            start = pulse[j][q] * 2 * RADIX_A
            halves = [x_ref[pl.ds(start + c, RADIX_A, stride=2), :] for c in range(2)]
            signal.append(jnp.concatenate(halves, axis=0))
        results.append(left_product(wa[...], jnp.concatenate(signal, axis=1)))
    for j in pairs:
        turned = []
        for q in range(2):
            part = results[j][:, q * RADIX_B : (q + 1) * RADIX_B]
            turned.append(jnp.concatenate(times(part[:RADIX_A], part[RADIX_A:], tw[0], tw[1]), axis=1))
        results[j] = right_product(jnp.concatenate(turned, axis=0), wb[...])
    for j in pairs:
        turned = []
        for q in range(2):
            part = results[j][q * RADIX_A : (q + 1) * RADIX_A]
            at = shift[j][q] + HALO
            gain = times(filt[0], filt[1], lanes[at, 0:1, :], lanes[at, 1:2, :])
            turned.append(jnp.concatenate(times(part[:, :RADIX_B], part[:, RADIX_B:], *gain), axis=1))
        results[j] = right_product(jnp.concatenate(turned, axis=0), vb[...])
    for j in pairs:
        turned = []
        for q in range(2):
            part = results[j][q * RADIX_A : (q + 1) * RADIX_A]
            at = shift[j][q] + HALO
            values = times(part[:, :RADIX_B], part[:, RADIX_B:], back[at, 0], back[at, 1])
            turned.append(jnp.concatenate(values, axis=0))
        results[j] = left_product(va[...], jnp.concatenate(turned, axis=1))
    bin8 = lax.broadcasted_iota(jnp.int32, (8, RADIX_B), 0) * RADIX_B
    bin8 = bin8 + lax.broadcasted_iota(jnp.int32, (8, RADIX_B), 1)
    for j in pairs:
        for q in range(2):
            s = shift[j][q]
            for c in range(2):
                values = results[j][c * RADIX_A : (c + 1) * RADIX_A, q * RADIX_B : (q + 1) * RADIX_B]
                top = jnp.where(bin8 + s >= 0, values[:8], 0.0)
                end = jnp.where(bin8 + s < 8 * RADIX_B, values[RADIX_A - 8 :], 0.0)
                values = jnp.concatenate([top, values[8 : RADIX_A - 8], end], axis=0)
                start = c * RADIX_A * PULSES + pulse[j][q]
                rows[pl.ds(start, RADIX_A, stride=PULSES), :] = values


def kernel(
    shift_hbm, x_hbm, f_hbm, steer_hbm, off_hbm, weight_hbm, rate_hbm,
    wa_hbm, wb_hbm, vb_hbm, va_hbm, tw_hbm, back_hbm, lanes_hbm, out_ref,
    shift_ref, x_ref, f_ref, steer_ref, off_ref, weight_ref, rate_ref, wa, wb, vb, va, tw, back, lanes,
    filt, rows, pulses, held, params, left, steer, band, phase, sent, image,
    load_sem, echo_sem, pulse_send, pulse_recv, param_send, param_recv, image_send, image_recv, tile_send, tile_recv,
    local_sem,
):
    sub = lax.axis_index("sub")
    rng = lax.axis_index("rng")
    barrier = pltpu.get_barrier_semaphore()
    for k in range(1, RANKS):
        pl.semaphore_signal(barrier, inc=1, device_id={"rng": lax.rem(rng + k, RANKS)}, device_id_type=MESH)
    for k in range(1, SUBS):
        pl.semaphore_signal(barrier, inc=1, device_id={"sub": lax.rem(sub + k, SUBS)}, device_id_type=MESH)

    step_rows = PAIRS * 4 * RADIX_A

    def echo_copy(i):
        part = pl.ds(pl.multiple_of(i * step_rows, step_rows), step_rows)
        return pltpu.make_async_copy(x_hbm.at[part], x_ref.at[part], echo_sem.at[i])

    def load(n, src, dst):
        return pltpu.make_async_copy(src, dst, load_sem.at[n])

    first_loads = [
        load(n, src, dst)
        for n, (src, dst) in enumerate(
            [(wa_hbm, wa), (tw_hbm, tw), (f_hbm, f_ref), (shift_hbm, shift_ref), (wb_hbm, wb), (vb_hbm, vb),
             (lanes_hbm, lanes), (va_hbm, va), (back_hbm, back)]
        )
    ]
    late_loads = [
        load(len(first_loads) + n, src, dst)
        for n, (src, dst) in enumerate(
            [(steer_hbm, steer_ref), (off_hbm, off_ref), (weight_hbm, weight_ref), (rate_hbm, rate_ref)]
        )
    ]
    echo_copy(0).start()
    for copy in first_loads:
        copy.start()
    for i in range(1, STEPS):
        echo_copy(i).start()
    for copy in late_loads:
        copy.start()
    for copy in first_loads:
        copy.wait()
    load_filter(f_ref, filt)

    def filter_step(i, carry):
        echo_copy(i).wait()
        compress(i, rng * PULSES, shift_ref, x_ref, filt, wa, wb, vb, va, tw, back, lanes, rows)
        return carry

    lax.fori_loop(0, STEPS, filter_step, 0)

    def pack(j, carry):
        for stage in range(STAGES):
            for c in range(2):
                start = (c * RADIX_A + j * ROWS + stage * STAGE_ROWS) * PULSES
                block = rows[pl.ds(pl.multiple_of(start, PULSES), STAGE_ROWS * PULSES), :].astype(BF16)
                pulses[stage, j, c] = block.reshape(STAGE_ROWS, PULSES, RADIX_B)
        return carry

    lax.fori_loop(0, RANKS, pack, 0)

    pl.semaphore_wait(barrier, RANKS + SUBS - 2)

    def pulse_copy(stage, src, dst, peer):
        return pltpu.make_async_remote_copy(
            src_ref=pulses.at[stage, src], dst_ref=held.at[stage, dst], send_sem=pulse_send.at[stage, src],
            recv_sem=pulse_recv.at[stage, dst], device_id={"rng": peer}, device_id_type=MESH,
        )

    def own_pulses(stage):
        return pltpu.make_async_copy(pulses.at[stage, rng], held.at[stage, rng], local_sem.at[stage])

    for stage in range(STAGES):

        def send_pulses(k, carry):
            peer = lax.rem(rng + k, RANKS)
            pulse_copy(stage, peer, rng, peer).start()
            return carry

        lax.fori_loop(1, RANKS, send_pulses, 0)
        own_pulses(stage).start()

    for copy in late_loads:
        copy.wait()
    for h in range(2):
        params[sub, 8 * h : 8 * h + 1, :] = off_ref[h : h + 1, :].astype(F32)
        params[sub, 8 * h + 1 : 8 * h + 5, :] = weight_ref[h]
        params[sub, 8 * h + 5 : 8 * h + 6, :] = rate_ref[h : h + 1, :]
        params[sub, 8 * h + 6 : 8 * h + 8, :] = jnp.zeros((2, ANGLES), F32)

    def param_copy(slot, peer):
        return pltpu.make_async_remote_copy(
            src_ref=params.at[slot], dst_ref=params.at[slot], send_sem=param_send.at[peer],
            recv_sem=param_recv.at[slot], device_id={"sub": peer}, device_id_type=MESH,
        )

    for k in range(1, SUBS):
        param_copy(sub, lax.rem(sub + k, SUBS)).start()

    real = steer_ref[0].astype(F32)
    imag = steer_ref[1].astype(F32)
    steer[:PSUB, :ANGLES] = real.T.astype(BF16)
    steer[:PSUB, ANGLES:] = imag.T.astype(BF16)
    steer[PSUB:, :ANGLES] = (-imag).T.astype(BF16)
    steer[PSUB:, ANGLES:] = real.T.astype(BF16)

    for k in range(1, SUBS):
        peer = lax.rem(sub + k, SUBS)
        param_copy(peer, peer).wait_recv()

    angle = lax.broadcasted_iota(jnp.int32, (1, ANGLES), 1).astype(F32)
    across = lax.broadcasted_iota(jnp.int32, (RADIX_B, ANGLES), 0).astype(F32)
    row8 = lax.broadcasted_iota(jnp.int32, (8, ANGLES), 0)
    base = rng * BLOCK + sub * PIECE

    def prepare(group, carry):
        for h in range(2):
            offset = params[group, 8 * h : 8 * h + 1, :]
            sources = [jnp.clip(angle + offset + float(t - 1), 0.0, ANGLES - 1.0) for t in range(TAPS)]
            weights = [params[group, 8 * h + 1 + t : 8 * h + 2 + t, :] for t in range(TAPS)]
            for part in range(ANGLES // RADIX_B):
                here = across + float(part * RADIX_B)
                total = jnp.zeros((RADIX_B, ANGLES), F32)
                for t in range(TAPS):
                    total = total + jnp.where(here == sources[t], weights[t], 0.0)
                band[2 * group + h, part * RADIX_B : (part + 1) * RADIX_B, :] = total.astype(BF16)
            rate = params[group, 8 * h + 5 : 8 * h + 6, :]
            by = jnp.broadcast_to(rate * (8.0 / SAMPLES), (8, ANGLES))
            sr, si = jnp.cos(by), jnp.sin(by)
            for stage in range(STAGES):
                at = rate * ((base + stage * STAGE_BINS + row8).astype(F32) / SAMPLES)
                pr, pi = jnp.cos(at), jnp.sin(at)
                for t in range(PIECE // 8):
                    part = slice(8 * t, 8 * t + 8)
                    qr, qi = pr, pi
                    for level in range(LEVELS):
                        phase[stage * LEVELS + level, 2 * group + h, 0, part, :] = qr
                        phase[stage * LEVELS + level, 2 * group + h, 1, part, :] = qi
                        if level < LEVELS - 1:
                            qr, qi = times(qr, qi, pr, pi)
                    if t < PIECE // 8 - 1:
                        pr, pi = times(pr, pi, sr, si)
        return carry

    lax.fori_loop(0, SUBS, prepare, 0)

    def image_copy(stage, src, dst, peer):
        return pltpu.make_async_remote_copy(
            src_ref=sent.at[stage, src], dst_ref=image.at[stage, 0, dst], send_sem=image_send.at[stage, src],
            recv_sem=image_recv.at[stage, dst], device_id={"sub": peer}, device_id_type=MESH,
        )

    def own_image(stage):
        return pltpu.make_async_copy(sent.at[stage, sub], image.at[stage, 0, sub], local_sem.at[STAGES + stage])

    for stage in range(STAGES):

        def pulses_here(k, carry):
            peer = lax.rem(rng + k, RANKS)
            pulse_copy(stage, peer, peer, peer).wait_recv()
            return carry

        lax.fori_loop(1, RANKS, pulses_here, 0)
        own_pulses(stage).wait()
        for row in range(STAGE_ROWS):
            for c in range(2):
                block = held[stage, :, c, row].reshape(PSUB, RADIX_B)
                left[stage, row * RADIX_B : (row + 1) * RADIX_B, c * PSUB : (c + 1) * PSUB] = block.T

        def make_image(k, carry):
            peer = lax.rem(sub + k, SUBS)
            bins = pl.ds(pl.multiple_of(peer * PIECE, PIECE), PIECE)
            part = dot(left[stage, bins, :], steer[...]).astype(BF16)
            for c in range(2):
                sent[stage, peer, c] = part[:, c * ANGLES : (c + 1) * ANGLES]

            @pl.when(k < SUBS)
            def _():
                image_copy(stage, peer, sub, peer).start()

            return carry

        lax.fori_loop(1, SUBS + 1, make_image, 0)
        own_image(stage).start()

    def tile_copy(stage, src, dst, peer):
        return pltpu.make_async_remote_copy(
            src_ref=image.at[stage, 1, src], dst_ref=out_ref.at[stage, dst], send_sem=tile_send.at[stage, src],
            recv_sem=tile_recv.at[stage, dst], device_id={"sub": peer}, device_id_type=MESH,
        )

    def own_tile(stage):
        return pltpu.make_async_copy(
            image.at[stage, 1, sub], out_ref.at[stage, sub], local_sem.at[2 * STAGES + stage]
        )

    for stage in range(STAGES):

        def image_here(k, carry):
            peer = lax.rem(sub + k, SUBS)
            image_copy(stage, peer, peer, peer).wait_recv()
            return carry

        lax.fori_loop(1, SUBS, image_here, 0)
        own_image(stage).wait()

        def merge(i, carry):
            level = i // SUBS
            k = lax.rem(i, SUBS) + 1
            group = lax.rem(sub + k, SUBS)
            now = lax.rem(level, 2)
            bit = 1 + level + level // 2
            far_group = group + bit - 2 * bit * lax.rem(group // bit, 2)
            turn = phase.at[stage * LEVELS + level]
            own = dot(image[stage, now, group].reshape(2 * PIECE, ANGLES), band[2 * group])
            far = dot(image[stage, now, far_group].reshape(2 * PIECE, ANGLES), band[2 * group + 1])
            ar, ai = times(own[:PIECE], own[PIECE:], turn[2 * group, 0], turn[2 * group, 1])
            br, bi = times(far[:PIECE], far[PIECE:], turn[2 * group + 1, 0], turn[2 * group + 1, 1])
            image[stage, 1 - now, group, 0] = (ar + br).astype(BF16)
            image[stage, 1 - now, group, 1] = (ai + bi).astype(BF16)

            @pl.when(jnp.logical_and(level == LEVELS - 1, k < SUBS))
            def _():
                tile_copy(stage, group, sub, group).start()

            return carry

        lax.fori_loop(0, LEVELS * SUBS, merge, 0)
        own_tile(stage).start()

    for stage in range(STAGES):

        def finish(k, carry):
            peer = lax.rem(sub + k, SUBS)
            tile_copy(stage, peer, peer, peer).wait_recv()
            tile_copy(stage, peer, sub, peer).wait_send()
            image_copy(stage, peer, sub, peer).wait_send()
            return carry

        lax.fori_loop(1, SUBS, finish, 0)
        own_tile(stage).wait()

        def pulses_gone(k, carry):
            peer = lax.rem(rng + k, RANKS)
            pulse_copy(stage, peer, rng, peer).wait_send()
            return carry

        lax.fori_loop(1, RANKS, pulses_gone, 0)
    for k in range(1, SUBS):
        param_copy(sub, lax.rem(sub + k, SUBS)).wait_send()


def tile_kernel(x_ref, out_ref):
    for stage in range(STAGES):
        for c in range(2):
            image = x_ref[stage, :, c].reshape(STAGE_BINS, ANGLES)
            for row in range(STAGE_ROWS):
                for part in range(ANGLES // RADIX_B):
                    angles = slice(part * RADIX_B, (part + 1) * RADIX_B)
                    start = stage * STAGE_BINS + row * RADIX_B
                    values = image[row * RADIX_B : (row + 1) * RADIX_B, angles]
                    out_ref[angles, c, start : start + RADIX_B] = values.astype(F32).T


def local(echoes, filter_spectrum, range_shifts, steering, tap_offsets, tap_weights, phase_rates):
    rows = echoes.reshape(PULSES, 2, RADIX_A, RADIX_B).transpose(0, 2, 1, 3).reshape(-1, RADIX_B)
    filt = filter_spectrum.reshape(2, RADIX_A, RADIX_B).transpose(1, 0, 2).reshape(-1, RADIX_B)
    consts = [jnp.asarray(t) for t in tables()]
    operands = [
        range_shifts,
        rows,
        filt,
        steering.reshape(2, ANGLES, PSUB),
        tap_offsets.reshape(2, ANGLES),
        tap_weights.reshape(2, TAPS, ANGLES),
        phase_rates.reshape(2, ANGLES),
        *consts,
    ]
    hbm = pl.BlockSpec(memory_space=pltpu.HBM)
    dma = pltpu.SemaphoreType.DMA
    landing = [pltpu.SMEM((PSUB,), jnp.int32)] + [pltpu.VMEM(x.shape, x.dtype) for x in operands[1:]]
    merged = pl.pallas_call(
        kernel,
        out_shape=jax.ShapeDtypeStruct((STAGES, SUBS, 2, PIECE, ANGLES), BF16),
        in_specs=[hbm] * len(operands),
        out_specs=hbm,
        scratch_shapes=[
            *landing,
            pltpu.VMEM((2, RADIX_A, RADIX_B), F32),
            pltpu.VMEM((2 * RADIX_A * PULSES, RADIX_B), F32),
            pltpu.VMEM((STAGES, RANKS, 2, STAGE_ROWS, PULSES, RADIX_B), BF16),
            pltpu.VMEM((STAGES, RANKS, 2, STAGE_ROWS, PULSES, RADIX_B), BF16),
            pltpu.VMEM((SUBS, PARAMS, ANGLES), F32),
            pltpu.VMEM((STAGES, STAGE_BINS, 2 * PSUB), BF16),
            pltpu.VMEM((2 * PSUB, 2 * ANGLES), BF16),
            pltpu.VMEM((2 * SUBS, ANGLES, ANGLES), BF16),
            pltpu.VMEM((STAGES * LEVELS, 2 * SUBS, 2, PIECE, ANGLES), F32),
            pltpu.VMEM((STAGES, SUBS, 2, PIECE, ANGLES), BF16),
            pltpu.VMEM((STAGES, 2, SUBS, 2, PIECE, ANGLES), BF16),
            dma((len(operands),)), dma((STEPS,)), dma((STAGES, RANKS)), dma((STAGES, RANKS)), dma((SUBS,)), dma((SUBS,)),
            dma((STAGES, SUBS)), dma((STAGES, SUBS)), dma((STAGES, SUBS)), dma((STAGES, SUBS)), dma((3 * STAGES,)),
        ],
        compiler_params=pltpu.CompilerParams(
            collective_id=0, has_side_effects=True, vmem_limit_bytes=56 << 20
        ),
        name="merge",
    )(*operands)
    vmem = pl.BlockSpec(memory_space=pltpu.VMEM)
    return pl.pallas_call(
        tile_kernel,
        out_shape=jax.ShapeDtypeStruct((ANGLES, 2, BLOCK), F32),
        in_specs=[vmem],
        out_specs=vmem,
        compiler_params=pltpu.CompilerParams(vmem_limit_bytes=32 << 20),
        name="tile",
    )(merged)


def solution(mesh):
    placed = (
        P(("sub", "rng"), None, None),
        P(),
        P("sub"),
        P("sub", None, None, None),
        P("sub", None, None),
        P("sub", None, None, None),
        P("sub", None, None),
    )
    return jax.shard_map(
        local, mesh=mesh, in_specs=placed, out_specs=P("sub", None, "rng"), check_vma=False
    )
```

```python
import math

import jax
import jax.numpy as jnp
import ml_dtypes
import numpy as np
from jax import lax
from jax.experimental import pallas as pl
from jax.experimental.pallas import tpu as pltpu
from jax.sharding import PartitionSpec as P

RADIX_A = 96
RADIX_B = 128
ANGLES = 384
TAPS = 4
SAMPLES = 12288
SUBS = 8
RANKS = 16
PULSES = 16
PSUB = RANKS * PULSES
BLOCK = SAMPLES // RANKS
ROWS = BLOCK // RADIX_B
STAGES = 2
STAGE_ROWS = ROWS // STAGES
STAGE_BINS = BLOCK // STAGES
PIECE = STAGE_BINS // SUBS
TOGETHER = 8
ECHO_PARTS = 4
HALO = 16
LEVELS = 3
PARAMS = 16
MESH = pl.DeviceIdType.MESH
F32 = jnp.float32
BF16 = jnp.bfloat16


def halves(table, axis):
    high = table.astype(np.float32).astype(ml_dtypes.bfloat16)
    low = (table - high.astype(np.float64)).astype(np.float32).astype(ml_dtypes.bfloat16)
    return np.concatenate([high, high, low], axis=axis)


def tables():
    a = np.arange(RADIX_A)
    b = np.arange(RADIX_B)
    wa = np.exp(-2j * np.pi / RADIX_A * (np.outer(a, a) % RADIX_A))
    wb = np.exp(-2j * np.pi / RADIX_B * (np.outer(b, b) % RADIX_B))
    order = 4 * (b % 32) + b // 32
    wb = wb[:, order]
    vb = np.conj(wb.T)
    va = np.conj(wa)
    left = lambda w: halves(np.block([[w.real, -w.imag], [w.imag, w.real]]), 1)
    right = lambda w: halves(np.block([[w.real, w.imag], [-w.imag, w.real]]), 0)
    turn = np.exp(-2j * np.pi / SAMPLES * np.outer(a, b))
    shifts = np.arange(-HALO, HALO + 1)
    back = np.exp(2j * np.pi / SAMPLES * a[None, :, None] * (b[None, None, :] + shifts[:, None, None])) / SAMPLES
    columns = np.exp(2j * np.pi / RADIX_B * (np.outer(shifts, order) % RADIX_B))
    lanes = np.zeros((2 * HALO + 1, 8, RADIX_B))
    lanes[:, 0], lanes[:, 1] = columns.real, columns.imag
    return (
        left(wa),
        right(wb),
        right(vb),
        left(va),
        np.stack([turn.real, turn.imag]).astype(np.float32),
        np.stack([back.real, back.imag], axis=1).astype(np.float32),
        lanes.astype(np.float32),
    )


def split(x):
    high = x.astype(BF16)
    return high, (x - high.astype(F32)).astype(BF16)


def dot(left, right):
    return jnp.dot(left, right, preferred_element_type=F32)


def left_product(table, x):
    high, low = split(x)
    return dot(table, jnp.concatenate([high, low, high], axis=0))


def right_product(x, table):
    high, low = split(x)
    return dot(jnp.concatenate([high, low, high], axis=1), table)


def times(ar, ai, br, bi):
    return ar * br - ai * bi, ar * bi + ai * br


def load_filter(f_ref, filt):
    lane32 = lax.broadcasted_iota(jnp.int32, (32, RADIX_B), 1)
    for c in range(2):
        f0, f1, f2 = (f_ref[pl.ds(2 * e + c, 32, stride=6), :] for e in range(3))
        parts = [
            f0,
            jnp.where(lane32 < 32, pltpu.roll(f0, 32, 1), pltpu.roll(f1, 32, 1)),
            jnp.where(lane32 < 64, pltpu.roll(f1, 64, 1), pltpu.roll(f2, 64, 1)),
            pltpu.roll(f2, 96, 1),
        ]
        filt[c] = jnp.concatenate(parts, axis=0).T[:RADIX_A]


def compress(first, arrived, shift_ref, x_ref, f_ref, filt, wa, wb, vb, va, tw, back, lanes, rows):
    pairs = range(PULSES // 2)
    pulse = [[2 * j + q for q in range(2)] for j in pairs]
    results = []
    arrived("wa")
    arrived("tw")
    for j in pairs:
        if j % 2 == 0:
            arrived(j // 2)
        signal = []
        for q in range(2):
            start = pulse[j][q] * 2 * RADIX_A
            halves = [x_ref[pl.ds(start + c, RADIX_A, stride=2), :] for c in range(2)]
            signal.append(jnp.concatenate(halves, axis=0))
        results.append(left_product(wa[...], jnp.concatenate(signal, axis=1)))
    arrived("wb")
    for j in pairs:
        turned = []
        for q in range(2):
            part = results[j][:, q * RADIX_B : (q + 1) * RADIX_B]
            turned.append(jnp.concatenate(times(part[:RADIX_A], part[RADIX_A:], tw[0], tw[1]), axis=1))
        results[j] = right_product(jnp.concatenate(turned, axis=0), wb[...])
    arrived("filter")
    arrived("shift")
    arrived("lanes")
    arrived("vb")
    load_filter(f_ref, filt)
    shift = [[shift_ref[first + p] for p in two] for two in pulse]
    for j in pairs:
        turned = []
        for q in range(2):
            part = results[j][q * RADIX_A : (q + 1) * RADIX_A]
            at = shift[j][q] + HALO
            gain = times(filt[0], filt[1], lanes[at, 0:1, :], lanes[at, 1:2, :])
            turned.append(jnp.concatenate(times(part[:, :RADIX_B], part[:, RADIX_B:], *gain), axis=1))
        results[j] = right_product(jnp.concatenate(turned, axis=0), vb[...])
    arrived("back")
    arrived("va")
    for j in pairs:
        turned = []
        for q in range(2):
            part = results[j][q * RADIX_A : (q + 1) * RADIX_A]
            at = shift[j][q] + HALO
            values = times(part[:, :RADIX_B], part[:, RADIX_B:], back[at, 0], back[at, 1])
            turned.append(jnp.concatenate(values, axis=0))
        results[j] = left_product(va[...], jnp.concatenate(turned, axis=1))
    bin8 = lax.broadcasted_iota(jnp.int32, (8, RADIX_B), 0) * RADIX_B
    bin8 = bin8 + lax.broadcasted_iota(jnp.int32, (8, RADIX_B), 1)
    for j in pairs:
        for q in range(2):
            s = shift[j][q]
            for c in range(2):
                values = results[j][c * RADIX_A : (c + 1) * RADIX_A, q * RADIX_B : (q + 1) * RADIX_B]
                top = jnp.where(bin8 + s >= 0, values[:8], 0.0)
                end = jnp.where(bin8 + s < 8 * RADIX_B, values[RADIX_A - 8 :], 0.0)
                values = jnp.concatenate([top, values[8 : RADIX_A - 8], end], axis=0)
                start = c * RADIX_A * PULSES + pulse[j][q]
                rows[pl.ds(start, RADIX_A, stride=PULSES), :] = values


def kernel(
    shift_hbm, x_hbm, f_hbm, steer_hbm, off_hbm, weight_hbm, rate_hbm,
    wa_hbm, wb_hbm, vb_hbm, va_hbm, tw_hbm, back_hbm, lanes_hbm, out_ref,
    shift_ref, x_ref, f_ref, steer_ref, off_ref, weight_ref, rate_ref, wa, wb, vb, va, tw, back, lanes,
    filt, rows, pulses, held, params, rates, turns, left, steer, band, phase, sent, image,
    load_sem, echo_sem, pulse_send, pulse_recv, param_send, param_recv, image_send, image_recv, tile_send, tile_recv,
    local_sem,
):
    sub = lax.axis_index("sub")
    rng = lax.axis_index("rng")
    barrier = pltpu.get_barrier_semaphore()
    for k in range(1, RANKS):
        pl.semaphore_signal(barrier, inc=1, device_id={"rng": lax.rem(rng + k, RANKS)}, device_id_type=MESH)
    for k in range(1, SUBS):
        pl.semaphore_signal(barrier, inc=1, device_id={"sub": lax.rem(sub + k, SUBS)}, device_id_type=MESH)

    echo_rows = x_ref.shape[0] // ECHO_PARTS

    def echo_copy(i):
        part = pl.ds(i * echo_rows, echo_rows)
        return pltpu.make_async_copy(x_hbm.at[part], x_ref.at[part], echo_sem.at[i])

    def load(n, src, dst):
        return pltpu.make_async_copy(src, dst, load_sem.at[n])

    names = ["wa", "tw", "wb", "filter", "shift", "lanes", "vb", "va", "back"]
    arrays = [
        (wa_hbm, wa), (tw_hbm, tw), (wb_hbm, wb), (f_hbm, f_ref), (shift_hbm, shift_ref), (lanes_hbm, lanes),
        (vb_hbm, vb), (va_hbm, va), (back_hbm, back), (steer_hbm, steer_ref), (off_hbm, off_ref),
        (weight_hbm, weight_ref), (rate_hbm, rate_ref),
    ]
    copies = [load(n, src, dst) for n, (src, dst) in enumerate(arrays)]
    late_loads = copies[len(names) :]
    loads = dict(zip(names, copies))
    loads.update({i: echo_copy(i) for i in range(ECHO_PARTS)})
    order = ["wa", 0, "tw", 1, "wb", 2, 3, "filter", "shift", "lanes", "vb", "va", "back"]
    for name in order:
        loads[name].start()
    for copy in late_loads:
        copy.start()

    def arrived(name):
        loads[name].wait()

    compress(rng * PULSES, arrived, shift_ref, x_ref, f_ref, filt, wa, wb, vb, va, tw, back, lanes, rows)

    def pack(j, carry):
        for stage in range(STAGES):
            for c in range(2):
                start = (c * RADIX_A + j * ROWS + stage * STAGE_ROWS) * PULSES
                block = rows[pl.ds(pl.multiple_of(start, PULSES), STAGE_ROWS * PULSES), :].astype(BF16)
                pulses[stage, j, c] = block.reshape(STAGE_ROWS, PULSES, RADIX_B)
        return carry

    lax.fori_loop(0, RANKS, pack, 0)

    pl.semaphore_wait(barrier, RANKS + SUBS - 2)

    def pulse_copy(stage, src, dst, peer):
        return pltpu.make_async_remote_copy(
            src_ref=pulses.at[stage, src], dst_ref=held.at[stage, dst], send_sem=pulse_send.at[stage, src],
            recv_sem=pulse_recv.at[stage, dst], device_id={"rng": peer}, device_id_type=MESH,
        )

    def own_pulses(stage):
        return pltpu.make_async_copy(pulses.at[stage, rng], held.at[stage, rng], local_sem.at[stage])

    for stage in range(STAGES):

        def send_pulses(k, carry):
            peer = lax.rem(rng + k, RANKS)
            pulse_copy(stage, peer, rng, peer).start()
            return carry

        lax.fori_loop(1, RANKS, send_pulses, 0)
        own_pulses(stage).start()

    def clear(which, carry):
        band[which] = jnp.zeros((2, 2 * RADIX_B, 2 * RADIX_B), BF16)
        return carry

    lax.fori_loop(0, 2 * SUBS, clear, 0)

    for copy in late_loads:
        copy.wait()
    for h in range(2):
        params[sub, 8 * h : 8 * h + 1, :] = off_ref[h : h + 1, :].astype(F32)
        params[sub, 8 * h + 1 : 8 * h + 5, :] = weight_ref[h]
        params[sub, 8 * h + 5 : 8 * h + 6, :] = rate_ref[h : h + 1, :]
        params[sub, 8 * h + 6 : 8 * h + 8, :] = jnp.zeros((2, ANGLES), F32)

    def param_copy(slot, peer):
        return pltpu.make_async_remote_copy(
            src_ref=params.at[slot], dst_ref=params.at[slot], send_sem=param_send.at[peer],
            recv_sem=param_recv.at[slot], device_id={"sub": peer}, device_id_type=MESH,
        )

    for k in range(1, SUBS):
        param_copy(sub, lax.rem(sub + k, SUBS)).start()

    real = steer_ref[0].astype(F32)
    imag = steer_ref[1].astype(F32)
    steer[:PSUB, :ANGLES] = real.T.astype(BF16)
    steer[:PSUB, ANGLES:] = imag.T.astype(BF16)
    steer[PSUB:, :ANGLES] = (-imag).T.astype(BF16)
    steer[PSUB:, ANGLES:] = real.T.astype(BF16)

    for k in range(1, SUBS):
        peer = lax.rem(sub + k, SUBS)
        param_copy(peer, peer).wait_recv()

    angle = lax.broadcasted_iota(jnp.int32, (1, ANGLES), 1).astype(F32)
    across = lax.broadcasted_iota(jnp.int32, (RADIX_B, RADIX_B), 0).astype(F32)
    row8 = lax.broadcasted_iota(jnp.int32, (8, ANGLES), 0)
    for group in range(SUBS):
        for h in range(2):
            rates[2 * group + h : 2 * group + h + 1, :] = params[group, 8 * h + 5 : 8 * h + 6, :]
    base = (rng * BLOCK + sub * PIECE).astype(F32)
    for n, bins in enumerate([base, 1.0, 2.0, 4.0, 8.0, float(STAGE_BINS)]):
        at = rates[...] * (bins / SAMPLES)
        turns[n, 0] = jnp.cos(at)
        turns[n, 1] = jnp.sin(at)

    def prepare(which, carry):
        group, h = which // 2, lax.rem(which, 2)
        own = params.at[group, pl.ds(pl.multiple_of(8 * h, 8), 8)]
        sources = [jnp.clip(angle + own[0:1, :] + float(t - 1), 0.0, ANGLES - 1.0) for t in range(TAPS)]
        weights = [own[1 + t : 2 + t, :] for t in range(TAPS)]

        lower = angle < float(ANGLES // 2)
        halved = [[jnp.where(lower == (block == 0), w, 0.0) for w in weights] for block in range(2)]

        def fill(block, first, count, part):
            lanes = slice(part * RADIX_B, (part + 1) * RADIX_B)
            here = across[:count] + float(first)
            total = jnp.zeros((count, RADIX_B), F32)
            for t in range(TAPS):
                total = total + jnp.where(here == sources[t][:, lanes], halved[block][t][:, lanes], 0.0)
            row, col = first - block * RADIX_B, (part - block) * RADIX_B
            band[which, block, row : row + count, col : col + RADIX_B] = total.astype(BF16)

        fill(0, 0, 128, 0)
        fill(0, 128, 16, 0)
        fill(0, 112, 16, 1)
        fill(0, 128, 80, 1)
        fill(1, 176, 80, 1)
        fill(1, 256, 16, 1)
        fill(1, 240, 16, 2)
        fill(1, 256, 128, 2)

        def turn(n):
            return tuple(turns[n, c, pl.ds(which, 1), :] for c in range(2))

        def chosen(n, bit):
            real, imag = turn(n)
            on = lax.rem(row8 // bit, 2) == 1
            return jnp.where(on, real, 1.0), jnp.where(on, imag, 0.0)

        start = times(*times(*times(*chosen(1, 1), *chosen(2, 2)), *chosen(3, 4)), *turn(0))
        by8, by_stage = turn(4), turn(5)
        for stage in range(STAGES):
            if stage:
                start = times(*start, *by_stage)
            at = start
            for t in range(PIECE // 8):
                part = slice(8 * t, 8 * t + 8)
                now = at
                for level in range(LEVELS):
                    phase[stage * LEVELS + level, which, 0, part, :] = now[0]
                    phase[stage * LEVELS + level, which, 1, part, :] = now[1]
                    if level < LEVELS - 1:
                        now = times(*now, *at)
                if t < PIECE // 8 - 1:
                    at = times(*at, *by8)
        return carry

    lax.fori_loop(0, 2 * SUBS, prepare, 0)

    def image_copy(stage, src, dst, peer):
        return pltpu.make_async_remote_copy(
            src_ref=sent.at[stage, src], dst_ref=image.at[stage, 0, dst], send_sem=image_send.at[stage, src],
            recv_sem=image_recv.at[stage, dst], device_id={"sub": peer}, device_id_type=MESH,
        )

    def own_image(stage):
        return pltpu.make_async_copy(sent.at[stage, sub], image.at[stage, 0, sub], local_sem.at[STAGES + stage])

    for stage in range(STAGES):

        def pulses_here(k, carry):
            peer = lax.rem(rng + k, RANKS)
            pulse_copy(stage, peer, peer, peer).wait_recv()
            return carry

        lax.fori_loop(1, RANKS, pulses_here, 0)
        own_pulses(stage).wait()
        for row in range(STAGE_ROWS):
            for c in range(2):
                block = held[stage, :, c, row].reshape(PSUB, RADIX_B)
                left[stage, row * RADIX_B : (row + 1) * RADIX_B, c * PSUB : (c + 1) * PSUB] = block.T

        parts = dot(left[stage], steer[...]).astype(BF16)
        for c in range(2):
            sent[stage, :, c] = parts[:, c * ANGLES : (c + 1) * ANGLES].reshape(SUBS, PIECE, ANGLES)

        def send_image(k, carry):
            peer = lax.rem(sub + k, SUBS)
            image_copy(stage, peer, sub, peer).start()
            return carry

        lax.fori_loop(1, SUBS, send_image, 0)
        own_image(stage).start()

    def resampled(values, which):
        values = values.reshape(2 * PIECE, ANGLES)
        low = dot(values[:, : 2 * RADIX_B], band[which, 0])
        high = dot(values[:, RADIX_B:], band[which, 1])
        middle = low[:, RADIX_B:] + high[:, :RADIX_B]
        return jnp.concatenate([low[:, :RADIX_B], middle, high[:, RADIX_B:]], axis=1)

    def tile_copy(stage, src, dst, peer):
        return pltpu.make_async_remote_copy(
            src_ref=image.at[stage, 1, src], dst_ref=out_ref.at[stage, dst], send_sem=tile_send.at[stage, src],
            recv_sem=tile_recv.at[stage, dst], device_id={"sub": peer}, device_id_type=MESH,
        )

    def own_tile(stage):
        return pltpu.make_async_copy(
            image.at[stage, 1, sub], out_ref.at[stage, sub], local_sem.at[2 * STAGES + stage]
        )

    for stage in range(STAGES):

        def image_here(k, carry):
            peer = lax.rem(sub + k, SUBS)
            image_copy(stage, peer, peer, peer).wait_recv()
            return carry

        lax.fori_loop(1, SUBS, image_here, 0)
        own_image(stage).wait()

        def merge(i, carry):
            level = i // (SUBS // TOGETHER)
            now = lax.rem(level, 2)
            bit = 1 + level + level // 2
            turn = phase.at[stage * LEVELS + level]
            last = lax.rem(i, SUBS // TOGETHER) * TOGETHER + 1
            groups = [lax.rem(sub + last + j, SUBS) for j in range(TOGETHER)]
            pairs = []
            for group in groups:
                far_group = group + bit - 2 * bit * lax.rem(group // bit, 2)
                own = resampled(image[stage, now, group], 2 * group)
                far = resampled(image[stage, now, far_group], 2 * group + 1)
                pairs.append((own, far))
            for group, (own, far) in zip(groups, pairs):
                ar, ai = times(own[:PIECE], own[PIECE:], turn[2 * group, 0], turn[2 * group, 1])
                br, bi = times(far[:PIECE], far[PIECE:], turn[2 * group + 1, 0], turn[2 * group + 1, 1])
                image[stage, 1 - now, group, 0] = (ar + br).astype(BF16)
                image[stage, 1 - now, group, 1] = (ai + bi).astype(BF16)

            @pl.when(level == LEVELS - 1)
            def _():
                for j, group in enumerate(groups):

                    @pl.when(last + j < SUBS)
                    def _():
                        tile_copy(stage, group, sub, group).start()

            return carry

        lax.fori_loop(0, LEVELS * SUBS // TOGETHER, merge, 0)
        own_tile(stage).start()

    for stage in range(STAGES):

        def finish(k, carry):
            peer = lax.rem(sub + k, SUBS)
            tile_copy(stage, peer, peer, peer).wait_recv()
            tile_copy(stage, peer, sub, peer).wait_send()
            image_copy(stage, peer, sub, peer).wait_send()
            return carry

        lax.fori_loop(1, SUBS, finish, 0)
        own_tile(stage).wait()

        def pulses_gone(k, carry):
            peer = lax.rem(rng + k, RANKS)
            pulse_copy(stage, peer, rng, peer).wait_send()
            return carry

        lax.fori_loop(1, RANKS, pulses_gone, 0)
    for k in range(1, SUBS):
        param_copy(sub, lax.rem(sub + k, SUBS)).wait_send()


def tile_kernel(x_ref, out_ref):
    for stage in range(STAGES):
        for c in range(2):
            image = x_ref[stage, :, c].reshape(STAGE_BINS, RADIX_B)
            for row in range(STAGE_ROWS):
                start = stage * STAGE_BINS + row * RADIX_B
                values = image[row * RADIX_B : (row + 1) * RADIX_B]
                out_ref[:, c, start : start + RADIX_B] = values.T.astype(F32)


def local(echoes, filter_spectrum, range_shifts, steering, tap_offsets, tap_weights, phase_rates):
    rows = echoes.reshape(PULSES, 2, RADIX_A, RADIX_B).transpose(0, 2, 1, 3).reshape(-1, RADIX_B)
    filt = filter_spectrum.reshape(2, RADIX_A, RADIX_B).transpose(1, 0, 2).reshape(-1, RADIX_B)
    consts = [jnp.asarray(t) for t in tables()]
    operands = [
        range_shifts,
        rows,
        filt,
        steering.reshape(2, ANGLES, PSUB),
        tap_offsets.reshape(2, ANGLES),
        tap_weights.reshape(2, TAPS, ANGLES),
        phase_rates.reshape(2, ANGLES),
        *consts,
    ]
    hbm = pl.BlockSpec(memory_space=pltpu.HBM)
    dma = pltpu.SemaphoreType.DMA
    landing = [pltpu.SMEM((PSUB,), jnp.int32)] + [pltpu.VMEM(x.shape, x.dtype) for x in operands[1:]]
    merged = pl.pallas_call(
        kernel,
        out_shape=jax.ShapeDtypeStruct((STAGES, SUBS, 2, PIECE, ANGLES), BF16),
        in_specs=[hbm] * len(operands),
        out_specs=hbm,
        scratch_shapes=[
            *landing,
            pltpu.VMEM((2, RADIX_A, RADIX_B), F32),
            pltpu.VMEM((2 * RADIX_A * PULSES, RADIX_B), F32),
            pltpu.VMEM((STAGES, RANKS, 2, STAGE_ROWS, PULSES, RADIX_B), BF16),
            pltpu.VMEM((STAGES, RANKS, 2, STAGE_ROWS, PULSES, RADIX_B), BF16),
            pltpu.VMEM((SUBS, PARAMS, ANGLES), F32),
            pltpu.VMEM((2 * SUBS, ANGLES), F32),
            pltpu.VMEM((6, 2, 2 * SUBS, ANGLES), F32),
            pltpu.VMEM((STAGES, STAGE_BINS, 2 * PSUB), BF16),
            pltpu.VMEM((2 * PSUB, 2 * ANGLES), BF16),
            pltpu.VMEM((2 * SUBS, 2, 2 * RADIX_B, 2 * RADIX_B), BF16),
            pltpu.VMEM((STAGES * LEVELS, 2 * SUBS, 2, PIECE, ANGLES), F32),
            pltpu.VMEM((STAGES, SUBS, 2, PIECE, ANGLES), BF16),
            pltpu.VMEM((STAGES, 2, SUBS, 2, PIECE, ANGLES), BF16),
            dma((len(operands),)), dma((ECHO_PARTS,)), dma((STAGES, RANKS)), dma((STAGES, RANKS)), dma((SUBS,)), dma((SUBS,)),
            dma((STAGES, SUBS)), dma((STAGES, SUBS)), dma((STAGES, SUBS)), dma((STAGES, SUBS)), dma((3 * STAGES,)),
        ],
        compiler_params=pltpu.CompilerParams(
            collective_id=0, has_side_effects=True, vmem_limit_bytes=56 << 20
        ),
        name="merge",
    )(*operands)
    return pl.pallas_call(
        tile_kernel,
        out_shape=jax.ShapeDtypeStruct((ANGLES, 2, BLOCK), F32),
        grid=(ANGLES // RADIX_B,),
        in_specs=[pl.BlockSpec((STAGES, SUBS, 2, PIECE, RADIX_B), lambda i: (0, 0, 0, 0, i))],
        out_specs=pl.BlockSpec((RADIX_B, 2, BLOCK), lambda i: (i, 0, 0)),
        compiler_params=pltpu.CompilerParams(vmem_limit_bytes=56 << 20),
        name="tile",
    )(merged)


def solution(mesh):
    placed = (
        P(("sub", "rng"), None, None),
        P(),
        P("sub"),
        P("sub", None, None, None),
        P("sub", None, None),
        P("sub", None, None, None),
        P("sub", None, None),
    )
    return jax.shard_map(
        local, mesh=mesh, in_specs=placed, out_specs=P("sub", None, "rng"), check_vma=False
    )
```

```python
import math

import jax
import jax.numpy as jnp
import ml_dtypes
import numpy as np
from jax import lax
from jax.experimental import pallas as pl
from jax.experimental.pallas import tpu as pltpu
from jax.sharding import PartitionSpec as P

RADIX_A = 96
RADIX_B = 128
ANGLES = 384
TAPS = 4
SAMPLES = 12288
SUBS = 8
RANKS = 16
PULSES = 16
PSUB = RANKS * PULSES
BLOCK = SAMPLES // RANKS
ROWS = BLOCK // RADIX_B
STAGES = 2
STAGE_ROWS = ROWS // STAGES
STAGE_BINS = BLOCK // STAGES
PIECE = STAGE_BINS // SUBS
ECHO_PARTS = 4
HALO = 16
LEVELS = 3
PARAMS = 16
IMAGE_ORDER = ((0, 1), (1, 0), (0, 3), (1, 2), (0, 2), (1, 1), (1, 3))
TILE_ORDER = ((0, 1), (1, 0), (0, 3), (1, 2), (0, 2), (1, 1), (1, 3))
TILE_ANGLES = 128
MESH = pl.DeviceIdType.MESH
F32 = jnp.float32
BF16 = jnp.bfloat16


def halves(table, axis):
    high = table.astype(np.float32).astype(ml_dtypes.bfloat16)
    low = (table - high.astype(np.float64)).astype(np.float32).astype(ml_dtypes.bfloat16)
    return np.concatenate([high, high, low], axis=axis)


def tables():
    a = np.arange(RADIX_A)
    b = np.arange(RADIX_B)
    wa = np.exp(-2j * np.pi / RADIX_A * (np.outer(a, a) % RADIX_A))
    wb = np.exp(-2j * np.pi / RADIX_B * (np.outer(b, b) % RADIX_B))
    order = 4 * (b % 32) + b // 32
    wb = wb[:, order]
    vb = np.conj(wb.T)
    va = np.conj(wa)
    left = lambda w: halves(np.block([[w.real, -w.imag], [w.imag, w.real]]), 1)
    right = lambda w: halves(np.block([[w.real, w.imag], [-w.imag, w.real]]), 0)
    turn = np.exp(-2j * np.pi / SAMPLES * np.outer(a, b))
    shifts = np.arange(-HALO, HALO + 1)
    back = np.exp(2j * np.pi / SAMPLES * a[None, :, None] * (b[None, None, :] + shifts[:, None, None])) / SAMPLES
    columns = np.exp(2j * np.pi / RADIX_B * (np.outer(shifts, order) % RADIX_B))
    lanes = np.zeros((2 * HALO + 1, 8, RADIX_B))
    lanes[:, 0], lanes[:, 1] = columns.real, columns.imag
    return (
        left(wa),
        right(wb),
        right(vb),
        left(va),
        np.stack([turn.real, turn.imag]).astype(np.float32),
        np.stack([back.real, back.imag], axis=1).astype(np.float32),
        lanes.astype(np.float32),
    )


def split(x):
    high = x.astype(BF16)
    return high, (x - high.astype(F32)).astype(BF16)


def dot(left, right):
    return jnp.dot(left, right, preferred_element_type=F32)


def left_product(table, x):
    high, low = split(x)
    return dot(table, jnp.concatenate([high, low, high], axis=0))


def right_product(x, table):
    high, low = split(x)
    return dot(jnp.concatenate([high, low, high], axis=1), table)


def times(ar, ai, br, bi):
    return ar * br - ai * bi, ar * bi + ai * br


def load_filter(f_ref, filt):
    lane32 = lax.broadcasted_iota(jnp.int32, (32, RADIX_B), 1)
    for c in range(2):
        f0, f1, f2 = (f_ref[pl.ds(2 * e + c, 32, stride=6), :] for e in range(3))
        parts = [
            f0,
            jnp.where(lane32 < 32, pltpu.roll(f0, 32, 1), pltpu.roll(f1, 32, 1)),
            jnp.where(lane32 < 64, pltpu.roll(f1, 64, 1), pltpu.roll(f2, 64, 1)),
            pltpu.roll(f2, 96, 1),
        ]
        filt[c] = jnp.concatenate(parts, axis=0).T[:RADIX_A]


def compress(first, arrived, shift_ref, x_ref, f_ref, filt, wa, wb, vb, va, tw, back, lanes, rows):
    pairs = range(PULSES // 2)
    pulse = [[2 * j + q for q in range(2)] for j in pairs]
    results = []
    arrived("wa")
    arrived("tw")
    for j in pairs:
        if j % 2 == 0:
            arrived(j // 2)
        signal = []
        for q in range(2):
            start = pulse[j][q] * 2 * RADIX_A
            halves = [x_ref[pl.ds(start + c, RADIX_A, stride=2), :] for c in range(2)]
            signal.append(jnp.concatenate(halves, axis=0))
        results.append(left_product(wa[...], jnp.concatenate(signal, axis=1)))
    arrived("wb")
    for j in pairs:
        turned = []
        for q in range(2):
            part = results[j][:, q * RADIX_B : (q + 1) * RADIX_B]
            turned.append(jnp.concatenate(times(part[:RADIX_A], part[RADIX_A:], tw[0], tw[1]), axis=1))
        results[j] = right_product(jnp.concatenate(turned, axis=0), wb[...])
    arrived("filter")
    arrived("shift")
    arrived("lanes")
    arrived("vb")
    load_filter(f_ref, filt)
    shift = [[shift_ref[first + p] for p in two] for two in pulse]
    for j in pairs:
        turned = []
        for q in range(2):
            part = results[j][q * RADIX_A : (q + 1) * RADIX_A]
            at = shift[j][q] + HALO
            gain = times(filt[0], filt[1], lanes[at, 0:1, :], lanes[at, 1:2, :])
            turned.append(jnp.concatenate(times(part[:, :RADIX_B], part[:, RADIX_B:], *gain), axis=1))
        results[j] = right_product(jnp.concatenate(turned, axis=0), vb[...])
    arrived("back")
    arrived("va")
    for j in pairs:
        turned = []
        for q in range(2):
            part = results[j][q * RADIX_A : (q + 1) * RADIX_A]
            at = shift[j][q] + HALO
            values = times(part[:, :RADIX_B], part[:, RADIX_B:], back[at, 0], back[at, 1])
            turned.append(jnp.concatenate(values, axis=0))
        results[j] = left_product(va[...], jnp.concatenate(turned, axis=1))
    bin8 = lax.broadcasted_iota(jnp.int32, (8, RADIX_B), 0) * RADIX_B
    bin8 = bin8 + lax.broadcasted_iota(jnp.int32, (8, RADIX_B), 1)
    for j in pairs:
        for q in range(2):
            s = shift[j][q]
            for c in range(2):
                values = results[j][c * RADIX_A : (c + 1) * RADIX_A, q * RADIX_B : (q + 1) * RADIX_B]
                top = jnp.where(bin8 + s >= 0, values[:8], 0.0)
                end = jnp.where(bin8 + s < 8 * RADIX_B, values[RADIX_A - 8 :], 0.0)
                values = jnp.concatenate([top, values[8 : RADIX_A - 8], end], axis=0)
                start = c * RADIX_A * PULSES + pulse[j][q]
                rows[pl.ds(start, RADIX_A, stride=PULSES), :] = values


def nth_peer(index, size, k):
    half = size // 2
    across = (size - k) // half
    step = lax.rem(k - across, half)
    return lax.rem(index // half + across, 2) * half + lax.rem(lax.rem(index, half) + step, half)


def kernel(
    shift_hbm, x_hbm, f_hbm, steer_hbm, off_hbm, weight_hbm, rate_hbm,
    wa_hbm, wb_hbm, vb_hbm, va_hbm, tw_hbm, back_hbm, lanes_hbm, out_ref,
    shift_ref, x_ref, f_ref, steer_ref, off_ref, weight_ref, rate_ref, wa, wb, vb, va, tw, back, lanes,
    filt, rows, pulses, held, params, rates, turns, left, steer, band, phase, sent, image,
    load_sem, echo_sem, pulse_send, pulse_recv, param_send, param_recv, image_send, image_recv, tile_send, tile_recv,
    local_sem,
):
    sub = lax.axis_index("sub")
    rng = lax.axis_index("rng")
    barrier = pltpu.get_barrier_semaphore()
    for k in range(1, RANKS):
        pl.semaphore_signal(barrier, inc=1, device_id={"rng": lax.rem(rng + k, RANKS)}, device_id_type=MESH)
    for k in range(1, SUBS):
        pl.semaphore_signal(barrier, inc=1, device_id={"sub": lax.rem(sub + k, SUBS)}, device_id_type=MESH)

    echo_rows = x_ref.shape[0] // ECHO_PARTS

    def echo_copy(i):
        part = pl.ds(i * echo_rows, echo_rows)
        return pltpu.make_async_copy(x_hbm.at[part], x_ref.at[part], echo_sem.at[i])

    def load(n, src, dst):
        return pltpu.make_async_copy(src, dst, load_sem.at[n])

    names = ["wa", "tw", "wb", "filter", "shift", "lanes", "vb", "va", "back"]
    arrays = [
        (wa_hbm, wa), (tw_hbm, tw), (wb_hbm, wb), (f_hbm, f_ref), (shift_hbm, shift_ref), (lanes_hbm, lanes),
        (vb_hbm, vb), (va_hbm, va), (back_hbm, back), (steer_hbm, steer_ref), (off_hbm, off_ref),
        (weight_hbm, weight_ref), (rate_hbm, rate_ref),
    ]
    copies = [load(n, src, dst) for n, (src, dst) in enumerate(arrays)]
    late_loads = copies[len(names) :]
    loads = dict(zip(names, copies))
    loads.update({i: echo_copy(i) for i in range(ECHO_PARTS)})
    order = ["wa", 0, "tw", 1, "wb", 2, 3, "filter", "shift", "lanes", "vb", "va", "back"]
    for name in order:
        loads[name].start()
    for copy in late_loads:
        copy.start()

    def arrived(name):
        loads[name].wait()

    compress(rng * PULSES, arrived, shift_ref, x_ref, f_ref, filt, wa, wb, vb, va, tw, back, lanes, rows)

    def pack(j, carry):
        for stage in range(STAGES):
            for c in range(2):
                start = (c * RADIX_A + j * ROWS + stage * STAGE_ROWS) * PULSES
                block = rows[pl.ds(pl.multiple_of(start, PULSES), STAGE_ROWS * PULSES), :].astype(BF16)
                pulses[stage, j, c] = block.reshape(STAGE_ROWS, PULSES, RADIX_B)
        return carry

    lax.fori_loop(0, RANKS, pack, 0)

    pl.semaphore_wait(barrier, RANKS + SUBS - 2)

    def pulse_copy(stage, src, dst, peer):
        return pltpu.make_async_remote_copy(
            src_ref=pulses.at[stage, src], dst_ref=held.at[stage, dst], send_sem=pulse_send.at[stage, src],
            recv_sem=pulse_recv.at[stage, dst], device_id={"rng": peer}, device_id_type=MESH,
        )

    def own_pulses(stage):
        return pltpu.make_async_copy(pulses.at[stage, rng], held.at[stage, rng], local_sem.at[stage])

    for stage in range(STAGES):

        def send_pulses(k, carry):
            peer = nth_peer(rng, RANKS, k)
            pulse_copy(stage, peer, rng, peer).start()
            return carry

        lax.fori_loop(1, RANKS, send_pulses, 0)
        own_pulses(stage).start()

    def clear(which, carry):
        band[which] = jnp.zeros((2, 2 * RADIX_B, 2 * RADIX_B), BF16)
        return carry

    lax.fori_loop(0, 2 * SUBS, clear, 0)

    for copy in late_loads:
        copy.wait()
    for h in range(2):
        params[sub, 8 * h : 8 * h + 1, :] = off_ref[h : h + 1, :].astype(F32)
        params[sub, 8 * h + 1 : 8 * h + 5, :] = weight_ref[h]
        params[sub, 8 * h + 5 : 8 * h + 6, :] = rate_ref[h : h + 1, :]
        params[sub, 8 * h + 6 : 8 * h + 8, :] = jnp.zeros((2, ANGLES), F32)

    def param_copy(slot, peer):
        return pltpu.make_async_remote_copy(
            src_ref=params.at[slot], dst_ref=params.at[slot], send_sem=param_send.at[peer],
            recv_sem=param_recv.at[slot], device_id={"sub": peer}, device_id_type=MESH,
        )

    for k in range(1, SUBS):
        param_copy(sub, lax.rem(sub + k, SUBS)).start()

    real = steer_ref[0].astype(F32)
    imag = steer_ref[1].astype(F32)
    steer[:PSUB, :ANGLES] = real.T.astype(BF16)
    steer[:PSUB, ANGLES:] = imag.T.astype(BF16)
    steer[PSUB:, :ANGLES] = (-imag).T.astype(BF16)
    steer[PSUB:, ANGLES:] = real.T.astype(BF16)

    for k in range(1, SUBS):
        peer = lax.rem(sub + k, SUBS)
        param_copy(peer, peer).wait_recv()

    angle = lax.broadcasted_iota(jnp.int32, (1, ANGLES), 1).astype(F32)
    across = lax.broadcasted_iota(jnp.int32, (RADIX_B, RADIX_B), 0).astype(F32)
    row8 = lax.broadcasted_iota(jnp.int32, (8, ANGLES), 0)
    for group in range(SUBS):
        for h in range(2):
            rates[2 * group + h : 2 * group + h + 1, :] = params[group, 8 * h + 5 : 8 * h + 6, :]
    base = (rng * BLOCK + sub * PIECE).astype(F32)
    for n, bins in enumerate([base, 1.0, 2.0, 4.0, 8.0, float(STAGE_BINS)]):
        at = rates[...] * (bins / SAMPLES)
        turns[n, 0] = jnp.cos(at)
        turns[n, 1] = jnp.sin(at)

    def prepare(which, carry):
        group, h = which // 2, lax.rem(which, 2)
        own = params.at[group, pl.ds(pl.multiple_of(8 * h, 8), 8)]
        sources = [jnp.clip(angle + own[0:1, :] + float(t - 1), 0.0, ANGLES - 1.0) for t in range(TAPS)]
        weights = [own[1 + t : 2 + t, :] for t in range(TAPS)]

        lower = angle < float(ANGLES // 2)
        halved = [[jnp.where(lower == (block == 0), w, 0.0) for w in weights] for block in range(2)]

        def fill(block, first, count, part):
            lanes = slice(part * RADIX_B, (part + 1) * RADIX_B)
            here = across[:count] + float(first)
            total = jnp.zeros((count, RADIX_B), F32)
            for t in range(TAPS):
                total = total + jnp.where(here == sources[t][:, lanes], halved[block][t][:, lanes], 0.0)
            row, col = first - block * RADIX_B, (part - block) * RADIX_B
            band[which, block, row : row + count, col : col + RADIX_B] = total.astype(BF16)

        fill(0, 0, 128, 0)
        fill(0, 128, 16, 0)
        fill(0, 112, 16, 1)
        fill(0, 128, 80, 1)
        fill(1, 176, 80, 1)
        fill(1, 256, 16, 1)
        fill(1, 240, 16, 2)
        fill(1, 256, 128, 2)

        def turn(n):
            return tuple(turns[n, c, pl.ds(which, 1), :] for c in range(2))

        def chosen(n, bit):
            real, imag = turn(n)
            on = lax.rem(row8 // bit, 2) == 1
            return jnp.where(on, real, 1.0), jnp.where(on, imag, 0.0)

        start = times(*times(*times(*chosen(1, 1), *chosen(2, 2)), *chosen(3, 4)), *turn(0))
        by8, by_stage = turn(4), turn(5)
        for stage in range(STAGES):
            if stage:
                start = times(*start, *by_stage)
            at = start
            for t in range(PIECE // 8):
                part = slice(8 * t, 8 * t + 8)
                now = at
                for level in range(LEVELS):
                    phase[stage * LEVELS + level, which, 0, part, :] = now[0]
                    phase[stage * LEVELS + level, which, 1, part, :] = now[1]
                    if level < LEVELS - 1:
                        now = times(*now, *at)
                if t < PIECE // 8 - 1:
                    at = times(*at, *by8)
        return carry

    lax.fori_loop(0, 2 * SUBS, prepare, 0)

    def across(flip, step):
        return lax.rem(sub // 4 + flip, 2) * 4 + lax.rem(lax.rem(sub, 4) + step, 4)

    def image_copy(stage, src, dst, peer):
        return pltpu.make_async_remote_copy(
            src_ref=sent.at[stage, src], dst_ref=image.at[stage, 0, dst], send_sem=image_send.at[stage, src],
            recv_sem=image_recv.at[stage, dst], device_id={"sub": peer}, device_id_type=MESH,
        )

    def own_image(stage):
        return pltpu.make_async_copy(sent.at[stage, sub], image.at[stage, 0, sub], local_sem.at[STAGES + stage])

    for stage in range(STAGES):

        def pulses_here(k, carry):
            peer = lax.rem(rng + k, RANKS)
            pulse_copy(stage, peer, peer, peer).wait_recv()
            return carry

        lax.fori_loop(1, RANKS, pulses_here, 0)
        own_pulses(stage).wait()
        for row in range(STAGE_ROWS):
            for c in range(2):
                block = held[stage, :, c, row].reshape(PSUB, RADIX_B)
                left[stage, row * RADIX_B : (row + 1) * RADIX_B, c * PSUB : (c + 1) * PSUB] = block.T

        parts = dot(left[stage], steer[...]).astype(BF16)
        for c in range(2):
            sent[stage, :, c] = parts[:, c * ANGLES : (c + 1) * ANGLES].reshape(SUBS, PIECE, ANGLES)

        for flip, step in IMAGE_ORDER:
            peer = across(flip, step)
            image_copy(stage, peer, sub, peer).start()
        own_image(stage).start()

    def resampled(values, which):
        values = values.reshape(2 * PIECE, ANGLES)
        low = dot(values[:, : 2 * RADIX_B], band[which, 0])
        high = dot(values[:, RADIX_B:], band[which, 1])
        middle = low[:, RADIX_B:] + high[:, :RADIX_B]
        return jnp.concatenate([low[:, :RADIX_B], middle, high[:, RADIX_B:]], axis=1)

    def tile_copy(stage, src, dst, peer):
        return pltpu.make_async_remote_copy(
            src_ref=image.at[stage, 1, src], dst_ref=out_ref.at[stage, dst], send_sem=tile_send.at[stage, src],
            recv_sem=tile_recv.at[stage, dst], device_id={"sub": peer}, device_id_type=MESH,
        )

    def own_tile(stage):
        return pltpu.make_async_copy(
            image.at[stage, 1, sub], out_ref.at[stage, sub], local_sem.at[2 * STAGES + stage]
        )

    for stage in range(STAGES):

        def image_here(k, carry):
            peer = lax.rem(sub + k, SUBS)
            image_copy(stage, peer, peer, peer).wait_recv()
            return carry

        lax.fori_loop(1, SUBS, image_here, 0)
        own_image(stage).wait()

        def merge(i, carry):
            level = i
            now = lax.rem(level, 2)
            bit = 1 + level + level // 2
            turn = phase.at[stage * LEVELS + level]
            groups = [across(flip, step) for flip, step in TILE_ORDER] + [sub]
            pairs = []
            for group in groups:
                far_group = group + bit - 2 * bit * lax.rem(group // bit, 2)
                own = resampled(image[stage, now, group], 2 * group)
                far = resampled(image[stage, now, far_group], 2 * group + 1)
                pairs.append((own, far))
            for group, (own, far) in zip(groups, pairs):
                ar, ai = times(own[:PIECE], own[PIECE:], turn[2 * group, 0], turn[2 * group, 1])
                br, bi = times(far[:PIECE], far[PIECE:], turn[2 * group + 1, 0], turn[2 * group + 1, 1])
                image[stage, 1 - now, group, 0] = (ar + br).astype(BF16)
                image[stage, 1 - now, group, 1] = (ai + bi).astype(BF16)

            @pl.when(level == LEVELS - 1)
            def _():
                for group in groups[:-1]:
                    tile_copy(stage, group, sub, group).start()

            return carry

        lax.fori_loop(0, LEVELS, merge, 0)
        own_tile(stage).start()

    for stage in range(STAGES):

        def finish(k, carry):
            peer = lax.rem(sub + k, SUBS)
            tile_copy(stage, peer, peer, peer).wait_recv()
            tile_copy(stage, peer, sub, peer).wait_send()
            image_copy(stage, peer, sub, peer).wait_send()
            return carry

        lax.fori_loop(1, SUBS, finish, 0)
        own_tile(stage).wait()

        def pulses_gone(k, carry):
            peer = lax.rem(rng + k, RANKS)
            pulse_copy(stage, peer, rng, peer).wait_send()
            return carry

        lax.fori_loop(1, RANKS, pulses_gone, 0)
    for k in range(1, SUBS):
        param_copy(sub, lax.rem(sub + k, SUBS)).wait_send()


def tile_kernel(x_hbm, out_hbm, x_ref, out_ref, in_sem, out_sem):
    def read(part):
        lanes = slice(part * RADIX_B, (part + 1) * RADIX_B)
        return pltpu.make_async_copy(x_hbm.at[:, :, :, :, lanes], x_ref.at[part], in_sem.at[part])

    def write(n):
        angles = pl.ds(n * TILE_ANGLES, TILE_ANGLES)
        return pltpu.make_async_copy(out_ref.at[angles], out_hbm.at[angles], out_sem.at[n])

    parts = ANGLES // RADIX_B
    for part in range(parts):
        read(part).start()
    for part in range(parts):
        read(part).wait()
        for piece in range(RADIX_B // TILE_ANGLES):
            lanes = slice(piece * TILE_ANGLES, (piece + 1) * TILE_ANGLES)
            n = part * (RADIX_B // TILE_ANGLES) + piece
            for stage in range(STAGES):
                for c in range(2):
                    image = x_ref[part, stage, :, c].reshape(STAGE_BINS, RADIX_B)
                    for row in range(STAGE_ROWS):
                        start = stage * STAGE_BINS + row * RADIX_B
                        values = image[row * RADIX_B : (row + 1) * RADIX_B].T[lanes]
                        out_ref[n * TILE_ANGLES : (n + 1) * TILE_ANGLES, c, start : start + RADIX_B] = values.astype(F32)
            write(n).start()
    for n in range(ANGLES // TILE_ANGLES):
        write(n).wait()


def local(echoes, filter_spectrum, range_shifts, steering, tap_offsets, tap_weights, phase_rates):
    rows = echoes.reshape(PULSES, 2, RADIX_A, RADIX_B).transpose(0, 2, 1, 3).reshape(-1, RADIX_B)
    filt = filter_spectrum.reshape(2, RADIX_A, RADIX_B).transpose(1, 0, 2).reshape(-1, RADIX_B)
    consts = [jnp.asarray(t) for t in tables()]
    operands = [
        range_shifts,
        rows,
        filt,
        steering.reshape(2, ANGLES, PSUB),
        tap_offsets.reshape(2, ANGLES),
        tap_weights.reshape(2, TAPS, ANGLES),
        phase_rates.reshape(2, ANGLES),
        *consts,
    ]
    hbm = pl.BlockSpec(memory_space=pltpu.HBM)
    dma = pltpu.SemaphoreType.DMA
    landing = [pltpu.SMEM((PSUB,), jnp.int32)] + [pltpu.VMEM(x.shape, x.dtype) for x in operands[1:]]
    merged = pl.pallas_call(
        kernel,
        out_shape=jax.ShapeDtypeStruct((STAGES, SUBS, 2, PIECE, ANGLES), BF16),
        in_specs=[hbm] * len(operands),
        out_specs=hbm,
        scratch_shapes=[
            *landing,
            pltpu.VMEM((2, RADIX_A, RADIX_B), F32),
            pltpu.VMEM((2 * RADIX_A * PULSES, RADIX_B), F32),
            pltpu.VMEM((STAGES, RANKS, 2, STAGE_ROWS, PULSES, RADIX_B), BF16),
            pltpu.VMEM((STAGES, RANKS, 2, STAGE_ROWS, PULSES, RADIX_B), BF16),
            pltpu.VMEM((SUBS, PARAMS, ANGLES), F32),
            pltpu.VMEM((2 * SUBS, ANGLES), F32),
            pltpu.VMEM((6, 2, 2 * SUBS, ANGLES), F32),
            pltpu.VMEM((STAGES, STAGE_BINS, 2 * PSUB), BF16),
            pltpu.VMEM((2 * PSUB, 2 * ANGLES), BF16),
            pltpu.VMEM((2 * SUBS, 2, 2 * RADIX_B, 2 * RADIX_B), BF16),
            pltpu.VMEM((STAGES * LEVELS, 2 * SUBS, 2, PIECE, ANGLES), F32),
            pltpu.VMEM((STAGES, SUBS, 2, PIECE, ANGLES), BF16),
            pltpu.VMEM((STAGES, 2, SUBS, 2, PIECE, ANGLES), BF16),
            dma((len(operands),)), dma((ECHO_PARTS,)), dma((STAGES, RANKS)), dma((STAGES, RANKS)), dma((SUBS,)), dma((SUBS,)),
            dma((STAGES, SUBS)), dma((STAGES, SUBS)), dma((STAGES, SUBS)), dma((STAGES, SUBS)), dma((3 * STAGES,)),
        ],
        compiler_params=pltpu.CompilerParams(
            collective_id=0, has_side_effects=True, vmem_limit_bytes=56 << 20
        ),
        name="merge",
    )(*operands)
    return pl.pallas_call(
        tile_kernel,
        out_shape=jax.ShapeDtypeStruct((ANGLES, 2, BLOCK), F32),
        in_specs=[hbm],
        out_specs=hbm,
        scratch_shapes=[
            pltpu.VMEM((ANGLES // RADIX_B, STAGES, SUBS, 2, PIECE, RADIX_B), BF16),
            pltpu.VMEM((ANGLES, 2, BLOCK), F32),
            dma((ANGLES // RADIX_B,)),
            dma((ANGLES // TILE_ANGLES,)),
        ],
        compiler_params=pltpu.CompilerParams(vmem_limit_bytes=56 << 20),
        name="tile",
    )(merged)


def solution(mesh):
    placed = (
        P(("sub", "rng"), None, None),
        P(),
        P("sub"),
        P("sub", None, None, None),
        P("sub", None, None),
        P("sub", None, None, None),
        P("sub", None, None),
    )
    return jax.shard_map(
        local, mesh=mesh, in_specs=placed, out_specs=P("sub", None, "rng"), check_vma=False
    )
```

```python
import math

import jax
import jax.numpy as jnp
import ml_dtypes
import numpy as np
from jax import lax
from jax.experimental import pallas as pl
from jax.experimental.pallas import tpu as pltpu
from jax.sharding import PartitionSpec as P

RADIX_A = 96
RADIX_B = 128
ANGLES = 384
TAPS = 4
SAMPLES = 12288
SUBS = 8
RANKS = 16
PULSES = 16
PSUB = RANKS * PULSES
BLOCK = SAMPLES // RANKS
ROWS = BLOCK // RADIX_B
STAGES = 2
STAGE_ROWS = ROWS // STAGES
STAGE_BINS = BLOCK // STAGES
PIECE = STAGE_BINS // SUBS
ECHO_PARTS = 4
HALO = 16
LEVELS = 3
PARAMS = 16
SPARE = 16
IMAGE_ORDER = ((0, 1), (1, 0), (0, 3), (1, 2), (0, 2), (1, 1), (1, 3))
TILE_ORDER = ((0, 1), (1, 0), (0, 3), (1, 2), (0, 2), (1, 1), (1, 3))
TILE_ANGLES = 128
MESH = pl.DeviceIdType.MESH
F32 = jnp.float32
BF16 = jnp.bfloat16


def halves(table, axis):
    high = table.astype(np.float32).astype(ml_dtypes.bfloat16)
    low = (table - high.astype(np.float64)).astype(np.float32).astype(ml_dtypes.bfloat16)
    return np.concatenate([high, high, low], axis=axis)


def tables():
    a = np.arange(RADIX_A)
    b = np.arange(RADIX_B)
    wa = np.exp(-2j * np.pi / RADIX_A * (np.outer(a, a) % RADIX_A))
    wb = np.exp(-2j * np.pi / RADIX_B * (np.outer(b, b) % RADIX_B))
    order = 4 * (b % 32) + b // 32
    wb = wb[:, order]
    vb = np.conj(wb.T)
    va = np.conj(wa)
    left = lambda w: halves(np.block([[w.real, -w.imag], [w.imag, w.real]]), 1)
    right = lambda w: halves(np.block([[w.real, w.imag], [-w.imag, w.real]]), 0)
    turn = np.exp(-2j * np.pi / SAMPLES * np.outer(a, b))
    shifts = np.arange(-HALO, HALO + 1)
    back = np.exp(2j * np.pi / SAMPLES * a[None, :, None] * (b[None, None, :] + shifts[:, None, None])) / SAMPLES
    columns = np.exp(2j * np.pi / RADIX_B * (np.outer(shifts, order) % RADIX_B))
    lanes = np.zeros((2 * HALO + 1, 8, RADIX_B))
    lanes[:, 0], lanes[:, 1] = columns.real, columns.imag
    return (
        left(wa),
        right(wb),
        right(vb),
        left(va),
        np.stack([turn.real, turn.imag]).astype(np.float32),
        np.stack([back.real, back.imag], axis=1).astype(np.float32),
        lanes.astype(np.float32),
    )


def split(x):
    high = x.astype(BF16)
    return high, (x - high.astype(F32)).astype(BF16)


def dot(left, right):
    return jnp.dot(left, right, preferred_element_type=F32)


def left_product(table, x):
    high, low = split(x)
    return dot(table, jnp.concatenate([high, low, high], axis=0))


def right_product(x, table):
    high, low = split(x)
    return dot(jnp.concatenate([high, low, high], axis=1), table)


def times(ar, ai, br, bi):
    return ar * br - ai * bi, ar * bi + ai * br


def load_filter(f_ref, filt):
    lane32 = lax.broadcasted_iota(jnp.int32, (32, RADIX_B), 1)
    for c in range(2):
        f0, f1, f2 = (f_ref[pl.ds(2 * e + c, 32, stride=6), :] for e in range(3))
        parts = [
            f0,
            jnp.where(lane32 < 32, pltpu.roll(f0, 32, 1), pltpu.roll(f1, 32, 1)),
            jnp.where(lane32 < 64, pltpu.roll(f1, 64, 1), pltpu.roll(f2, 64, 1)),
            pltpu.roll(f2, 96, 1),
        ]
        filt[c] = jnp.concatenate(parts, axis=0).T[:RADIX_A]


def compress(first, arrived, shift_ref, x_ref, f_ref, filt, wa, wb, vb, va, tw, back, lanes, rows):
    pairs = range(PULSES // 2)
    pulse = [[2 * j + q for q in range(2)] for j in pairs]
    results = []
    arrived("wa")
    arrived("tw")
    for j in pairs:
        if j % 2 == 0:
            arrived(j // 2)
        signal = []
        for q in range(2):
            start = pulse[j][q] * 2 * RADIX_A
            halves = [x_ref[pl.ds(start + c, RADIX_A, stride=2), :] for c in range(2)]
            signal.append(jnp.concatenate(halves, axis=0))
        results.append(left_product(wa[...], jnp.concatenate(signal, axis=1)))
    arrived("wb")
    for j in pairs:
        turned = []
        for q in range(2):
            part = results[j][:, q * RADIX_B : (q + 1) * RADIX_B]
            turned.append(jnp.concatenate(times(part[:RADIX_A], part[RADIX_A:], tw[0], tw[1]), axis=1))
        results[j] = right_product(jnp.concatenate(turned, axis=0), wb[...])
    arrived("filter")
    arrived("shift")
    arrived("lanes")
    arrived("vb")
    load_filter(f_ref, filt)
    shift = [[shift_ref[first + p] for p in two] for two in pulse]
    for j in pairs:
        turned = []
        for q in range(2):
            part = results[j][q * RADIX_A : (q + 1) * RADIX_A]
            at = shift[j][q] + HALO
            gain = times(filt[0], filt[1], lanes[at, 0:1, :], lanes[at, 1:2, :])
            turned.append(jnp.concatenate(times(part[:, :RADIX_B], part[:, RADIX_B:], *gain), axis=1))
        results[j] = right_product(jnp.concatenate(turned, axis=0), vb[...])
    arrived("back")
    arrived("va")
    for j in pairs:
        turned = []
        for q in range(2):
            part = results[j][q * RADIX_A : (q + 1) * RADIX_A]
            at = shift[j][q] + HALO
            values = times(part[:, :RADIX_B], part[:, RADIX_B:], back[at, 0], back[at, 1])
            turned.append(jnp.concatenate(values, axis=0))
        results[j] = left_product(va[...], jnp.concatenate(turned, axis=1))
    bin8 = lax.broadcasted_iota(jnp.int32, (8, RADIX_B), 0) * RADIX_B
    bin8 = bin8 + lax.broadcasted_iota(jnp.int32, (8, RADIX_B), 1)
    for j in pairs:
        for q in range(2):
            s = shift[j][q]
            for c in range(2):
                values = results[j][c * RADIX_A : (c + 1) * RADIX_A, q * RADIX_B : (q + 1) * RADIX_B]
                top = jnp.where(bin8 + s >= 0, values[:8], 0.0)
                end = jnp.where(bin8 + s < 8 * RADIX_B, values[RADIX_A - 8 :], 0.0)
                values = jnp.concatenate([top, values[8 : RADIX_A - 8], end], axis=0)
                start = c * RADIX_A * PULSES + pulse[j][q]
                rows[pl.ds(start, RADIX_A, stride=PULSES), :] = values


def nth_peer(index, size, k):
    half = size // 2
    across = (size - k) // half
    step = lax.rem(k - across, half)
    return lax.rem(index // half + across, 2) * half + lax.rem(lax.rem(index, half) + step, half)


def kernel(
    shift_hbm, x_hbm, f_hbm, steer_hbm, off_hbm, weight_hbm, rate_hbm,
    wa_hbm, wb_hbm, vb_hbm, va_hbm, tw_hbm, back_hbm, lanes_hbm, out_ref,
    shift_ref, x_ref, f_ref, steer_ref, off_ref, weight_ref, rate_ref, wa, wb, vb, va, tw, back, lanes,
    filt, rows, pulses, held, params, rates, turns, left, steer, band, phase, sent, image,
    load_sem, echo_sem, pulse_send, pulse_recv, param_send, param_recv, image_send, image_recv, tile_send, tile_recv,
    local_sem,
):
    sub = lax.axis_index("sub")
    rng = lax.axis_index("rng")
    barrier = pltpu.get_barrier_semaphore()
    for k in range(1, RANKS):
        pl.semaphore_signal(barrier, inc=1, device_id={"rng": lax.rem(rng + k, RANKS)}, device_id_type=MESH)
    for k in range(1, SUBS):
        pl.semaphore_signal(barrier, inc=1, device_id={"sub": lax.rem(sub + k, SUBS)}, device_id_type=MESH)

    echo_rows = x_hbm.shape[0] // ECHO_PARTS

    def echo_copy(i):
        part = pl.ds(i * echo_rows, echo_rows)
        return pltpu.make_async_copy(x_hbm.at[part], x_ref.at[part], echo_sem.at[i])

    def load(n, src, dst):
        return pltpu.make_async_copy(src, dst, load_sem.at[n])

    names = ["wa", "tw", "wb", "filter", "shift", "lanes", "vb", "va", "back"]
    arrays = [
        (wa_hbm, wa), (tw_hbm, tw), (wb_hbm, wb), (f_hbm, f_ref.at[pl.ds(0, 2 * RADIX_A)]), (shift_hbm, shift_ref), (lanes_hbm, lanes),
        (vb_hbm, vb), (va_hbm, va), (back_hbm, back), (steer_hbm, steer_ref), (off_hbm, off_ref),
        (weight_hbm, weight_ref), (rate_hbm, rate_ref),
    ]
    copies = [load(n, src, dst) for n, (src, dst) in enumerate(arrays)]
    late_loads = copies[len(names) :]
    loads = dict(zip(names, copies))
    loads.update({i: echo_copy(i) for i in range(ECHO_PARTS)})
    order = ["wa", 0, "tw", 1, "wb", 2, 3, "filter", "shift", "lanes", "vb", "va", "back"]
    for name in order:
        loads[name].start()
    for copy in late_loads:
        copy.start()

    def arrived(name):
        loads[name].wait()

    compress(rng * PULSES, arrived, shift_ref, x_ref, f_ref, filt, wa, wb, vb, va, tw, back, lanes, rows)

    def pack(j, carry):
        for stage in range(STAGES):
            for c in range(2):
                start = (c * RADIX_A + j * ROWS + stage * STAGE_ROWS) * PULSES
                block = rows[pl.ds(pl.multiple_of(start, PULSES), STAGE_ROWS * PULSES), :].astype(BF16)
                pulses[stage, j, c] = block.reshape(STAGE_ROWS, PULSES, RADIX_B)
        return carry

    lax.fori_loop(0, RANKS, pack, 0)

    pl.semaphore_wait(barrier, RANKS + SUBS - 2)

    def pulse_copy(stage, src, dst, peer):
        return pltpu.make_async_remote_copy(
            src_ref=pulses.at[stage, src], dst_ref=held.at[stage, dst], send_sem=pulse_send.at[stage, src],
            recv_sem=pulse_recv.at[stage, dst], device_id={"rng": peer}, device_id_type=MESH,
        )

    def own_pulses(stage):
        return pltpu.make_async_copy(pulses.at[stage, rng], held.at[stage, rng], local_sem.at[stage])

    for stage in range(STAGES):

        def send_pulses(k, carry):
            peer = nth_peer(rng, RANKS, k)
            pulse_copy(stage, peer, rng, peer).start()
            return carry

        lax.fori_loop(1, RANKS, send_pulses, 0)
        own_pulses(stage).start()

    def clear(which, carry):
        band[which] = jnp.zeros((2, 2 * RADIX_B, 2 * RADIX_B), BF16)
        return carry

    lax.fori_loop(0, 2 * SUBS, clear, 0)

    for copy in late_loads:
        copy.wait()
    for h in range(2):
        params[sub, 8 * h : 8 * h + 1, :] = off_ref[h : h + 1, :].astype(F32)
        params[sub, 8 * h + 1 : 8 * h + 5, :] = weight_ref[h]
        params[sub, 8 * h + 5 : 8 * h + 6, :] = rate_ref[h : h + 1, :]
        params[sub, 8 * h + 6 : 8 * h + 8, :] = jnp.zeros((2, ANGLES), F32)

    def param_copy(slot, peer):
        return pltpu.make_async_remote_copy(
            src_ref=params.at[slot], dst_ref=params.at[slot], send_sem=param_send.at[peer],
            recv_sem=param_recv.at[slot], device_id={"sub": peer}, device_id_type=MESH,
        )

    for k in range(1, SUBS):
        param_copy(sub, lax.rem(sub + k, SUBS)).start()

    real = steer_ref[0].astype(F32)
    imag = steer_ref[1].astype(F32)
    steer[:PSUB, :ANGLES] = real.T.astype(BF16)
    steer[:PSUB, ANGLES:] = imag.T.astype(BF16)
    steer[PSUB:, :ANGLES] = (-imag).T.astype(BF16)
    steer[PSUB:, ANGLES:] = real.T.astype(BF16)

    for k in range(1, SUBS):
        peer = lax.rem(sub + k, SUBS)
        param_copy(peer, peer).wait_recv()

    angle = lax.broadcasted_iota(jnp.int32, (1, ANGLES), 1).astype(F32)
    across = lax.broadcasted_iota(jnp.int32, (RADIX_B, RADIX_B), 0).astype(F32)
    row8 = lax.broadcasted_iota(jnp.int32, (8, ANGLES), 0)
    for group in range(SUBS):
        for h in range(2):
            rates[2 * group + h : 2 * group + h + 1, :] = params[group, 8 * h + 5 : 8 * h + 6, :]
    base = (rng * BLOCK + sub * PIECE).astype(F32)
    for n, bins in enumerate([base, 1.0, 2.0, 4.0, 8.0, float(STAGE_BINS)]):
        at = rates[...] * (bins / SAMPLES)
        turns[n, 0] = jnp.cos(at)
        turns[n, 1] = jnp.sin(at)

    def prepare(which, carry):
        group, h = which // 2, lax.rem(which, 2)
        own = params.at[group, pl.ds(pl.multiple_of(8 * h, 8), 8)]
        sources = [jnp.clip(angle + own[0:1, :] + float(t - 1), 0.0, ANGLES - 1.0) for t in range(TAPS)]
        weights = [own[1 + t : 2 + t, :] for t in range(TAPS)]

        lower = angle < float(ANGLES // 2)
        halved = [[jnp.where(lower == (block == 0), w, 0.0) for w in weights] for block in range(2)]

        def fill(block, first, count, part):
            lanes = slice(part * RADIX_B, (part + 1) * RADIX_B)
            here = across[:count] + float(first)
            total = jnp.zeros((count, RADIX_B), F32)
            for t in range(TAPS):
                total = total + jnp.where(here == sources[t][:, lanes], halved[block][t][:, lanes], 0.0)
            row, col = first - block * RADIX_B, (part - block) * RADIX_B
            band[which, block, row : row + count, col : col + RADIX_B] = total.astype(BF16)

        fill(0, 0, 128, 0)
        fill(0, 128, 16, 0)
        fill(0, 112, 16, 1)
        fill(0, 128, 80, 1)
        fill(1, 176, 80, 1)
        fill(1, 256, 16, 1)
        fill(1, 240, 16, 2)
        fill(1, 256, 128, 2)

        def turn(n):
            return tuple(turns[n, c, pl.ds(which, 1), :] for c in range(2))

        def chosen(n, bit):
            real, imag = turn(n)
            on = lax.rem(row8 // bit, 2) == 1
            return jnp.where(on, real, 1.0), jnp.where(on, imag, 0.0)

        start = times(*times(*times(*chosen(1, 1), *chosen(2, 2)), *chosen(3, 4)), *turn(0))
        by8, by_stage = turn(4), turn(5)
        for stage in range(STAGES):
            if stage:
                start = times(*start, *by_stage)
            at = start
            for t in range(PIECE // 8):
                part = slice(8 * t, 8 * t + 8)
                now = at
                for level in range(LEVELS):
                    phase[stage * LEVELS + level, which, 0, part, :] = now[0]
                    phase[stage * LEVELS + level, which, 1, part, :] = now[1]
                    if level < LEVELS - 1:
                        now = times(*now, *at)
                if t < PIECE // 8 - 1:
                    at = times(*at, *by8)
        return carry

    lax.fori_loop(0, 2 * SUBS, prepare, 0)

    def across(flip, step):
        return lax.rem(sub // 4 + flip, 2) * 4 + lax.rem(lax.rem(sub, 4) + step, 4)

    def image_copy(stage, src, dst, peer):
        return pltpu.make_async_remote_copy(
            src_ref=sent.at[stage, src], dst_ref=image.at[stage, 0, dst], send_sem=image_send.at[stage, src],
            recv_sem=image_recv.at[stage, dst], device_id={"sub": peer}, device_id_type=MESH,
        )

    def own_image(stage):
        return pltpu.make_async_copy(sent.at[stage, sub], image.at[stage, 0, sub], local_sem.at[STAGES + stage])

    for stage in range(STAGES):

        def pulses_here(k, carry):
            peer = lax.rem(rng + k, RANKS)
            pulse_copy(stage, peer, peer, peer).wait_recv()
            return carry

        lax.fori_loop(1, RANKS, pulses_here, 0)
        own_pulses(stage).wait()
        for row in range(STAGE_ROWS):
            for c in range(2):
                block = held[stage, :, c, row].reshape(PSUB, RADIX_B)
                left[stage, row * RADIX_B : (row + 1) * RADIX_B, c * PSUB : (c + 1) * PSUB] = block.T

        parts = dot(left[stage], steer[...]).astype(BF16)
        for c in range(2):
            sent[stage, :, c] = parts[:, c * ANGLES : (c + 1) * ANGLES].reshape(SUBS, PIECE, ANGLES)

        for flip, step in IMAGE_ORDER:
            peer = across(flip, step)
            image_copy(stage, peer, sub, peer).start()
        own_image(stage).start()

    def resampled(values, which):
        values = values.reshape(2 * PIECE, ANGLES)
        low = dot(values[:, : 2 * RADIX_B], band[which, 0])
        high = dot(values[:, RADIX_B:], band[which, 1])
        middle = low[:, RADIX_B:] + high[:, :RADIX_B]
        return jnp.concatenate([low[:, :RADIX_B], middle, high[:, RADIX_B:]], axis=1)

    def tile_copy(stage, src, dst, peer):
        return pltpu.make_async_remote_copy(
            src_ref=image.at[stage, 1, src], dst_ref=out_ref.at[stage, dst], send_sem=tile_send.at[stage, src],
            recv_sem=tile_recv.at[stage, dst], device_id={"sub": peer}, device_id_type=MESH,
        )

    def own_tile(stage):
        return pltpu.make_async_copy(
            image.at[stage, 1, sub], out_ref.at[stage, sub], local_sem.at[2 * STAGES + stage]
        )

    for stage in range(STAGES):

        def image_here(k, carry):
            peer = lax.rem(sub + k, SUBS)
            image_copy(stage, peer, peer, peer).wait_recv()
            return carry

        lax.fori_loop(1, SUBS, image_here, 0)
        own_image(stage).wait()

        def merge(i, carry):
            level = i
            now = lax.rem(level, 2)
            bit = 1 + level + level // 2
            turn = phase.at[stage * LEVELS + level]
            groups = [across(flip, step) for flip, step in TILE_ORDER] + [sub]
            pairs = []
            for group in groups:
                far_group = group + bit - 2 * bit * lax.rem(group // bit, 2)
                own = resampled(image[stage, now, group], 2 * group)
                far = resampled(image[stage, now, far_group], 2 * group + 1)
                pairs.append((own, far))
            for group, (own, far) in zip(groups, pairs):
                ar, ai = times(own[:PIECE], own[PIECE:], turn[2 * group, 0], turn[2 * group, 1])
                br, bi = times(far[:PIECE], far[PIECE:], turn[2 * group + 1, 0], turn[2 * group + 1, 1])
                image[stage, 1 - now, group, 0] = (ar + br).astype(BF16)
                image[stage, 1 - now, group, 1] = (ai + bi).astype(BF16)

            @pl.when(level == LEVELS - 1)
            def _():
                for group in groups[:-1]:
                    tile_copy(stage, group, sub, group).start()

            return carry

        lax.fori_loop(0, LEVELS, merge, 0)
        own_tile(stage).start()

    for stage in range(STAGES):

        def finish(k, carry):
            peer = lax.rem(sub + k, SUBS)
            tile_copy(stage, peer, peer, peer).wait_recv()
            tile_copy(stage, peer, sub, peer).wait_send()
            image_copy(stage, peer, sub, peer).wait_send()
            return carry

        lax.fori_loop(1, SUBS, finish, 0)
        own_tile(stage).wait()

        def pulses_gone(k, carry):
            peer = lax.rem(rng + k, RANKS)
            pulse_copy(stage, peer, rng, peer).wait_send()
            return carry

        lax.fori_loop(1, RANKS, pulses_gone, 0)
    for k in range(1, SUBS):
        param_copy(sub, lax.rem(sub + k, SUBS)).wait_send()


def tile_kernel(x_hbm, out_hbm, x_ref, out_ref, in_sem, out_sem):
    def read(part):
        lanes = slice(part * RADIX_B, (part + 1) * RADIX_B)
        return pltpu.make_async_copy(x_hbm.at[:, :, :, :, lanes], x_ref.at[part], in_sem.at[part])

    def write(n):
        angles = pl.ds(n * TILE_ANGLES, TILE_ANGLES)
        return pltpu.make_async_copy(out_ref.at[angles], out_hbm.at[angles], out_sem.at[n])

    parts = ANGLES // RADIX_B
    for part in range(parts):
        read(part).start()
    for part in range(parts):
        read(part).wait()
        for piece in range(RADIX_B // TILE_ANGLES):
            lanes = slice(piece * TILE_ANGLES, (piece + 1) * TILE_ANGLES)
            n = part * (RADIX_B // TILE_ANGLES) + piece
            for stage in range(STAGES):
                for c in range(2):
                    image = x_ref[part, stage, :, c].reshape(STAGE_BINS, RADIX_B)
                    for row in range(STAGE_ROWS):
                        start = stage * STAGE_BINS + row * RADIX_B
                        values = image[row * RADIX_B : (row + 1) * RADIX_B].T[lanes]
                        out_ref[n * TILE_ANGLES : (n + 1) * TILE_ANGLES, c, start : start + RADIX_B] = values.astype(F32)
            write(n).start()
    for n in range(ANGLES // TILE_ANGLES):
        write(n).wait()


def local(echoes, filter_spectrum, range_shifts, steering, tap_offsets, tap_weights, phase_rates):
    rows = echoes.reshape(PULSES, 2, RADIX_A, RADIX_B).transpose(0, 2, 1, 3).reshape(-1, RADIX_B)
    filt = filter_spectrum.reshape(2, RADIX_A, RADIX_B).transpose(1, 0, 2).reshape(-1, RADIX_B)
    consts = [jnp.asarray(t) for t in tables()]
    operands = [
        range_shifts,
        rows,
        filt,
        steering.reshape(2, ANGLES, PSUB),
        tap_offsets.reshape(2, ANGLES),
        tap_weights.reshape(2, TAPS, ANGLES),
        phase_rates.reshape(2, ANGLES),
        *consts,
    ]
    hbm = pl.BlockSpec(memory_space=pltpu.HBM)
    dma = pltpu.SemaphoreType.DMA
    landing = [
        pltpu.SMEM((PSUB,), jnp.int32),
        pltpu.VMEM((rows.shape[0] + SPARE, RADIX_B), F32),
        pltpu.VMEM((filt.shape[0] + SPARE, RADIX_B), F32),
    ] + [pltpu.VMEM(x.shape, x.dtype) for x in operands[3:]]
    merged = pl.pallas_call(
        kernel,
        out_shape=jax.ShapeDtypeStruct((STAGES, SUBS, 2, PIECE, ANGLES), BF16),
        in_specs=[hbm] * len(operands),
        out_specs=hbm,
        scratch_shapes=[
            *landing,
            pltpu.VMEM((2, RADIX_A, RADIX_B), F32),
            pltpu.VMEM((2 * RADIX_A * PULSES + SPARE, RADIX_B), F32),
            pltpu.VMEM((STAGES, RANKS, 2, STAGE_ROWS, PULSES, RADIX_B), BF16),
            pltpu.VMEM((STAGES, RANKS, 2, STAGE_ROWS, PULSES, RADIX_B), BF16),
            pltpu.VMEM((SUBS, PARAMS, ANGLES), F32),
            pltpu.VMEM((2 * SUBS, ANGLES), F32),
            pltpu.VMEM((6, 2, 2 * SUBS, ANGLES), F32),
            pltpu.VMEM((STAGES, STAGE_BINS, 2 * PSUB), BF16),
            pltpu.VMEM((2 * PSUB, 2 * ANGLES), BF16),
            pltpu.VMEM((2 * SUBS, 2, 2 * RADIX_B, 2 * RADIX_B), BF16),
            pltpu.VMEM((STAGES * LEVELS, 2 * SUBS, 2, PIECE, ANGLES), F32),
            pltpu.VMEM((STAGES, SUBS, 2, PIECE, ANGLES), BF16),
            pltpu.VMEM((STAGES, 2, SUBS, 2, PIECE, ANGLES), BF16),
            dma((len(operands),)), dma((ECHO_PARTS,)), dma((STAGES, RANKS)), dma((STAGES, RANKS)), dma((SUBS,)), dma((SUBS,)),
            dma((STAGES, SUBS)), dma((STAGES, SUBS)), dma((STAGES, SUBS)), dma((STAGES, SUBS)), dma((3 * STAGES,)),
        ],
        compiler_params=pltpu.CompilerParams(
            collective_id=0, has_side_effects=True, vmem_limit_bytes=56 << 20
        ),
        name="merge",
    )(*operands)
    return pl.pallas_call(
        tile_kernel,
        out_shape=jax.ShapeDtypeStruct((ANGLES, 2, BLOCK), F32),
        in_specs=[hbm],
        out_specs=hbm,
        scratch_shapes=[
            pltpu.VMEM((ANGLES // RADIX_B, STAGES, SUBS, 2, PIECE, RADIX_B), BF16),
            pltpu.VMEM((ANGLES, 2, BLOCK), F32),
            dma((ANGLES // RADIX_B,)),
            dma((ANGLES // TILE_ANGLES,)),
        ],
        compiler_params=pltpu.CompilerParams(vmem_limit_bytes=56 << 20),
        name="tile",
    )(merged)


def solution(mesh):
    placed = (
        P(("sub", "rng"), None, None),
        P(),
        P("sub"),
        P("sub", None, None, None),
        P("sub", None, None),
        P("sub", None, None, None),
        P("sub", None, None),
    )
    return jax.shard_map(
        local, mesh=mesh, in_specs=placed, out_specs=P("sub", None, "rng"), check_vma=False
    )
```

```python
import math

import jax
import jax.numpy as jnp
import ml_dtypes
import numpy as np
from jax import lax
from jax.experimental import pallas as pl
from jax.experimental.pallas import tpu as pltpu
from jax.sharding import PartitionSpec as P

RADIX_A = 96
RADIX_B = 128
ANGLES = 384
TAPS = 4
SAMPLES = 12288
SUBS = 8
RANKS = 16
PULSES = 16
PSUB = RANKS * PULSES
BLOCK = SAMPLES // RANKS
ROWS = BLOCK // RADIX_B
STAGES = 2
STAGE_ROWS = ROWS // STAGES
STAGE_BINS = BLOCK // STAGES
PIECE = STAGE_BINS // SUBS
ECHO_PARTS = 8
HALO = 16
LEVELS = 3
PARAMS = 16
SPARE = 16
IMAGE_ORDER = ((0, 1), (1, 0), (0, 3), (1, 2), (0, 2), (1, 1), (1, 3))
TILE_ORDER = ((0, 1), (1, 0), (0, 3), (1, 2), (0, 2), (1, 1), (1, 3))
TILE_ANGLES = 64
MESH = pl.DeviceIdType.MESH
F32 = jnp.float32
BF16 = jnp.bfloat16


def halves(table, axis):
    high = table.astype(np.float32).astype(ml_dtypes.bfloat16)
    low = (table - high.astype(np.float64)).astype(np.float32).astype(ml_dtypes.bfloat16)
    return np.concatenate([high, high, low], axis=axis)


def tables():
    a = np.arange(RADIX_A)
    b = np.arange(RADIX_B)
    wa = np.exp(-2j * np.pi / RADIX_A * (np.outer(a, a) % RADIX_A))
    wb = np.exp(-2j * np.pi / RADIX_B * (np.outer(b, b) % RADIX_B))
    order = 4 * (b % 32) + b // 32
    wb = wb[:, order]
    vb = np.conj(wb.T)
    va = np.conj(wa)
    left = lambda w: halves(np.block([[w.real, -w.imag], [w.imag, w.real]]), 1)
    right = lambda w: halves(np.block([[w.real, w.imag], [-w.imag, w.real]]), 0)
    turn = np.exp(-2j * np.pi / SAMPLES * np.outer(a, b))
    shifts = np.arange(-HALO, HALO + 1)
    back = np.exp(2j * np.pi / SAMPLES * a[None, :, None] * (b[None, None, :] + shifts[:, None, None])) / SAMPLES
    columns = np.exp(2j * np.pi / RADIX_B * (np.outer(shifts, order) % RADIX_B))
    lanes = np.zeros((2 * HALO + 1, 8, RADIX_B))
    lanes[:, 0], lanes[:, 1] = columns.real, columns.imag
    return (
        left(wa),
        right(wb),
        right(vb),
        left(va),
        np.stack([turn.real, turn.imag]).astype(np.float32),
        np.stack([back.real, back.imag], axis=1).astype(np.float32),
        lanes.astype(np.float32),
    )


def split(x):
    high = x.astype(BF16)
    return high, (x - high.astype(F32)).astype(BF16)


def dot(left, right):
    return jnp.dot(left, right, preferred_element_type=F32)


def left_product(table, x):
    high, low = split(x)
    return dot(table, jnp.concatenate([high, low, high], axis=0))


def right_product(x, table):
    high, low = split(x)
    return dot(jnp.concatenate([high, low, high], axis=1), table)


def times(ar, ai, br, bi):
    return ar * br - ai * bi, ar * bi + ai * br


def load_filter(f_ref, filt):
    lane32 = lax.broadcasted_iota(jnp.int32, (32, RADIX_B), 1)
    for c in range(2):
        f0, f1, f2 = (f_ref[pl.ds(2 * e + c, 32, stride=6), :] for e in range(3))
        parts = [
            f0,
            jnp.where(lane32 < 32, pltpu.roll(f0, 32, 1), pltpu.roll(f1, 32, 1)),
            jnp.where(lane32 < 64, pltpu.roll(f1, 64, 1), pltpu.roll(f2, 64, 1)),
            pltpu.roll(f2, 96, 1),
        ]
        filt[c] = jnp.concatenate(parts, axis=0).T[:RADIX_A]


def compress(first, arrived, shift_ref, x_ref, f_ref, filt, wa, wb, vb, va, tw, back, lanes, rows):
    pairs = range(PULSES // 2)
    pulse = [[2 * j + q for q in range(2)] for j in pairs]
    results = []
    arrived("wa")
    arrived("tw")
    for j in pairs:
        arrived(j)
        signal = []
        for q in range(2):
            start = pulse[j][q] * 2 * RADIX_A
            halves = [x_ref[pl.ds(start + c, RADIX_A, stride=2), :] for c in range(2)]
            signal.append(jnp.concatenate(halves, axis=0))
        results.append(left_product(wa[...], jnp.concatenate(signal, axis=1)))
    arrived("wb")
    for j in pairs:
        turned = []
        for q in range(2):
            part = results[j][:, q * RADIX_B : (q + 1) * RADIX_B]
            turned.append(jnp.concatenate(times(part[:RADIX_A], part[RADIX_A:], tw[0], tw[1]), axis=1))
        results[j] = right_product(jnp.concatenate(turned, axis=0), wb[...])
    arrived("filter")
    arrived("shift")
    arrived("lanes")
    arrived("vb")
    load_filter(f_ref, filt)
    shift = [[shift_ref[first + p] for p in two] for two in pulse]
    for j in pairs:
        turned = []
        for q in range(2):
            part = results[j][q * RADIX_A : (q + 1) * RADIX_A]
            at = shift[j][q] + HALO
            gain = times(filt[0], filt[1], lanes[at, 0:1, :], lanes[at, 1:2, :])
            turned.append(jnp.concatenate(times(part[:, :RADIX_B], part[:, RADIX_B:], *gain), axis=1))
        results[j] = right_product(jnp.concatenate(turned, axis=0), vb[...])
    arrived("back")
    arrived("va")
    for j in pairs:
        turned = []
        for q in range(2):
            part = results[j][q * RADIX_A : (q + 1) * RADIX_A]
            at = shift[j][q] + HALO
            values = times(part[:, :RADIX_B], part[:, RADIX_B:], back[at, 0], back[at, 1])
            turned.append(jnp.concatenate(values, axis=0))
        results[j] = left_product(va[...], jnp.concatenate(turned, axis=1))
    bin8 = lax.broadcasted_iota(jnp.int32, (8, RADIX_B), 0) * RADIX_B
    bin8 = bin8 + lax.broadcasted_iota(jnp.int32, (8, RADIX_B), 1)
    for j in pairs:
        for q in range(2):
            s = shift[j][q]
            for c in range(2):
                values = results[j][c * RADIX_A : (c + 1) * RADIX_A, q * RADIX_B : (q + 1) * RADIX_B]
                top = jnp.where(bin8 + s >= 0, values[:8], 0.0)
                end = jnp.where(bin8 + s < 8 * RADIX_B, values[RADIX_A - 8 :], 0.0)
                values = jnp.concatenate([top, values[8 : RADIX_A - 8], end], axis=0)
                start = c * RADIX_A * PULSES + pulse[j][q]
                rows[pl.ds(start, RADIX_A, stride=PULSES), :] = values


def nth_peer(index, size, k):
    half = size // 2
    across = (size - k) // half
    step = lax.rem(k - across, half)
    return lax.rem(index // half + across, 2) * half + lax.rem(lax.rem(index, half) + step, half)


def kernel(
    shift_hbm, x_hbm, f_hbm, steer_hbm, off_hbm, weight_hbm, rate_hbm,
    wa_hbm, wb_hbm, vb_hbm, va_hbm, tw_hbm, back_hbm, lanes_hbm, out_ref,
    shift_ref, x_ref, f_ref, steer_ref, off_ref, weight_ref, rate_ref, wa, wb, vb, va, tw, back, lanes,
    filt, rows, pulses, held, params, rates, turns, left, steer, band, phase, sent, image,
    load_sem, echo_sem, pulse_send, pulse_recv, param_send, param_recv, image_send, image_recv, tile_send, tile_recv,
    local_sem,
):
    sub = lax.axis_index("sub")
    rng = lax.axis_index("rng")
    barrier = pltpu.get_barrier_semaphore()
    for k in range(1, RANKS):
        pl.semaphore_signal(barrier, inc=1, device_id={"rng": lax.rem(rng + k, RANKS)}, device_id_type=MESH)
    for k in range(1, SUBS):
        pl.semaphore_signal(barrier, inc=1, device_id={"sub": lax.rem(sub + k, SUBS)}, device_id_type=MESH)

    echo_rows = x_hbm.shape[0] // ECHO_PARTS

    def echo_copy(i):
        part = pl.ds(i * echo_rows, echo_rows)
        return pltpu.make_async_copy(x_hbm.at[part], x_ref.at[part], echo_sem.at[i])

    def load(n, src, dst):
        return pltpu.make_async_copy(src, dst, load_sem.at[n])

    names = ["wa", "tw", "wb", "filter", "shift", "lanes", "vb", "va", "back"]
    arrays = [
        (wa_hbm, wa), (tw_hbm, tw), (wb_hbm, wb), (f_hbm, f_ref.at[pl.ds(0, 2 * RADIX_A)]), (shift_hbm, shift_ref), (lanes_hbm, lanes),
        (vb_hbm, vb), (va_hbm, va), (back_hbm, back), (steer_hbm, steer_ref), (off_hbm, off_ref),
        (weight_hbm, weight_ref), (rate_hbm, rate_ref),
    ]
    copies = [load(n, src, dst) for n, (src, dst) in enumerate(arrays)]
    late_loads = copies[len(names) :]
    loads = dict(zip(names, copies))
    loads.update({i: echo_copy(i) for i in range(ECHO_PARTS)})
    order = [0, "wa", 1, "tw", 2, 3, "wb", 4, 5, 6, 7, "filter", "shift", "lanes", "vb", "va", "back"]
    for name in order:
        loads[name].start()
    for copy in late_loads:
        copy.start()

    def arrived(name):
        loads[name].wait()

    compress(rng * PULSES, arrived, shift_ref, x_ref, f_ref, filt, wa, wb, vb, va, tw, back, lanes, rows)

    def pack(j, carry):
        for stage in range(STAGES):
            for c in range(2):
                start = (c * RADIX_A + j * ROWS + stage * STAGE_ROWS) * PULSES
                block = rows[pl.ds(pl.multiple_of(start, PULSES), STAGE_ROWS * PULSES), :].astype(BF16)
                pulses[stage, j, c] = block.reshape(STAGE_ROWS, PULSES, RADIX_B)
        return carry

    lax.fori_loop(0, RANKS, pack, 0)

    pl.semaphore_wait(barrier, RANKS + SUBS - 2)

    def pulse_copy(stage, src, dst, peer):
        return pltpu.make_async_remote_copy(
            src_ref=pulses.at[stage, src], dst_ref=held.at[stage, dst], send_sem=pulse_send.at[stage, src],
            recv_sem=pulse_recv.at[stage, dst], device_id={"rng": peer}, device_id_type=MESH,
        )

    def own_pulses(stage):
        return pltpu.make_async_copy(pulses.at[stage, rng], held.at[stage, rng], local_sem.at[stage])

    for stage in range(STAGES):

        def send_pulses(k, carry):
            peer = nth_peer(rng, RANKS, k)
            pulse_copy(stage, peer, rng, peer).start()
            return carry

        lax.fori_loop(1, RANKS, send_pulses, 0)
        own_pulses(stage).start()

    def clear(which, carry):
        band[which] = jnp.zeros((2, 2 * RADIX_B, 2 * RADIX_B), BF16)
        return carry

    lax.fori_loop(0, 2 * SUBS, clear, 0)

    for copy in late_loads:
        copy.wait()
    for h in range(2):
        params[sub, 8 * h : 8 * h + 1, :] = off_ref[h : h + 1, :].astype(F32)
        params[sub, 8 * h + 1 : 8 * h + 5, :] = weight_ref[h]
        params[sub, 8 * h + 5 : 8 * h + 6, :] = rate_ref[h : h + 1, :]
        params[sub, 8 * h + 6 : 8 * h + 8, :] = jnp.zeros((2, ANGLES), F32)

    def param_copy(slot, peer):
        return pltpu.make_async_remote_copy(
            src_ref=params.at[slot], dst_ref=params.at[slot], send_sem=param_send.at[peer],
            recv_sem=param_recv.at[slot], device_id={"sub": peer}, device_id_type=MESH,
        )

    for k in range(1, SUBS):
        param_copy(sub, lax.rem(sub + k, SUBS)).start()

    real = steer_ref[0].astype(F32)
    imag = steer_ref[1].astype(F32)
    steer[:PSUB, :ANGLES] = real.T.astype(BF16)
    steer[:PSUB, ANGLES:] = imag.T.astype(BF16)
    steer[PSUB:, :ANGLES] = (-imag).T.astype(BF16)
    steer[PSUB:, ANGLES:] = real.T.astype(BF16)

    for k in range(1, SUBS):
        peer = lax.rem(sub + k, SUBS)
        param_copy(peer, peer).wait_recv()

    angle = lax.broadcasted_iota(jnp.int32, (1, ANGLES), 1).astype(F32)
    across = lax.broadcasted_iota(jnp.int32, (RADIX_B, RADIX_B), 0).astype(F32)
    row8 = lax.broadcasted_iota(jnp.int32, (8, ANGLES), 0)
    for group in range(SUBS):
        for h in range(2):
            rates[2 * group + h : 2 * group + h + 1, :] = params[group, 8 * h + 5 : 8 * h + 6, :]
    base = (rng * BLOCK + sub * PIECE).astype(F32)
    for n, bins in enumerate([base, 1.0, 2.0, 4.0, 8.0, float(STAGE_BINS)]):
        at = rates[...] * (bins / SAMPLES)
        turns[n, 0] = jnp.cos(at)
        turns[n, 1] = jnp.sin(at)

    def prepare(which, carry):
        group, h = which // 2, lax.rem(which, 2)
        own = params.at[group, pl.ds(pl.multiple_of(8 * h, 8), 8)]
        sources = [jnp.clip(angle + own[0:1, :] + float(t - 1), 0.0, ANGLES - 1.0) for t in range(TAPS)]
        weights = [own[1 + t : 2 + t, :] for t in range(TAPS)]

        lower = angle < float(ANGLES // 2)
        halved = [[jnp.where(lower == (block == 0), w, 0.0) for w in weights] for block in range(2)]

        def fill(block, first, count, part):
            lanes = slice(part * RADIX_B, (part + 1) * RADIX_B)
            here = across[:count] + float(first)
            total = jnp.zeros((count, RADIX_B), F32)
            for t in range(TAPS):
                total = total + jnp.where(here == sources[t][:, lanes], halved[block][t][:, lanes], 0.0)
            row, col = first - block * RADIX_B, (part - block) * RADIX_B
            band[which, block, row : row + count, col : col + RADIX_B] = total.astype(BF16)

        fill(0, 0, 128, 0)
        fill(0, 128, 16, 0)
        fill(0, 112, 16, 1)
        fill(0, 128, 80, 1)
        fill(1, 176, 80, 1)
        fill(1, 256, 16, 1)
        fill(1, 240, 16, 2)
        fill(1, 256, 128, 2)

        def turn(n):
            return tuple(turns[n, c, pl.ds(which, 1), :] for c in range(2))

        def chosen(n, bit):
            real, imag = turn(n)
            on = lax.rem(row8 // bit, 2) == 1
            return jnp.where(on, real, 1.0), jnp.where(on, imag, 0.0)

        start = times(*times(*times(*chosen(1, 1), *chosen(2, 2)), *chosen(3, 4)), *turn(0))
        by8, by_stage = turn(4), turn(5)
        for stage in range(STAGES):
            if stage:
                start = times(*start, *by_stage)
            at = start
            for t in range(PIECE // 8):
                part = slice(8 * t, 8 * t + 8)
                now = at
                for level in range(LEVELS):
                    phase[stage * LEVELS + level, which, 0, part, :] = now[0]
                    phase[stage * LEVELS + level, which, 1, part, :] = now[1]
                    if level < LEVELS - 1:
                        now = times(*now, *at)
                if t < PIECE // 8 - 1:
                    at = times(*at, *by8)
        return carry

    lax.fori_loop(0, 2 * SUBS, prepare, 0)

    def across(flip, step):
        return lax.rem(sub // 4 + flip, 2) * 4 + lax.rem(lax.rem(sub, 4) + step, 4)

    def image_copy(stage, src, dst, peer):
        return pltpu.make_async_remote_copy(
            src_ref=sent.at[stage, src], dst_ref=image.at[stage, 0, dst], send_sem=image_send.at[stage, src],
            recv_sem=image_recv.at[stage, dst], device_id={"sub": peer}, device_id_type=MESH,
        )

    def own_image(stage):
        return pltpu.make_async_copy(sent.at[stage, sub], image.at[stage, 0, sub], local_sem.at[STAGES + stage])

    for stage in range(STAGES):

        def pulses_here(k, carry):
            peer = lax.rem(rng + k, RANKS)
            pulse_copy(stage, peer, peer, peer).wait_recv()
            return carry

        lax.fori_loop(1, RANKS, pulses_here, 0)
        own_pulses(stage).wait()
        for row in range(STAGE_ROWS):
            for c in range(2):
                block = held[stage, :, c, row].reshape(PSUB, RADIX_B)
                left[stage, row * RADIX_B : (row + 1) * RADIX_B, c * PSUB : (c + 1) * PSUB] = block.T

        parts = dot(left[stage], steer[...]).astype(BF16)
        for c in range(2):
            sent[stage, :, c] = parts[:, c * ANGLES : (c + 1) * ANGLES].reshape(SUBS, PIECE, ANGLES)

        for flip, step in IMAGE_ORDER:
            peer = across(flip, step)
            image_copy(stage, peer, sub, peer).start()
        own_image(stage).start()

    def resampled(values, which):
        values = values.reshape(2 * PIECE, ANGLES)
        low = dot(values[:, : 2 * RADIX_B], band[which, 0])
        high = dot(values[:, RADIX_B:], band[which, 1])
        middle = low[:, RADIX_B:] + high[:, :RADIX_B]
        return jnp.concatenate([low[:, :RADIX_B], middle, high[:, RADIX_B:]], axis=1)

    def tile_copy(stage, src, dst, peer):
        return pltpu.make_async_remote_copy(
            src_ref=image.at[stage, 1, src], dst_ref=out_ref.at[stage, dst], send_sem=tile_send.at[stage, src],
            recv_sem=tile_recv.at[stage, dst], device_id={"sub": peer}, device_id_type=MESH,
        )

    def own_tile(stage):
        return pltpu.make_async_copy(
            image.at[stage, 1, sub], out_ref.at[stage, sub], local_sem.at[2 * STAGES + stage]
        )

    for stage in range(STAGES):

        def image_here(k, carry):
            peer = lax.rem(sub + k, SUBS)
            image_copy(stage, peer, peer, peer).wait_recv()
            return carry

        lax.fori_loop(1, SUBS, image_here, 0)
        own_image(stage).wait()

        def merge(i, carry):
            level = i
            now = lax.rem(level, 2)
            bit = 1 + level + level // 2
            turn = phase.at[stage * LEVELS + level]
            groups = [across(flip, step) for flip, step in TILE_ORDER] + [sub]
            pairs = []
            for group in groups:
                far_group = group + bit - 2 * bit * lax.rem(group // bit, 2)
                own = resampled(image[stage, now, group], 2 * group)
                far = resampled(image[stage, now, far_group], 2 * group + 1)
                pairs.append((own, far))
            for group, (own, far) in zip(groups, pairs):
                ar, ai = times(own[:PIECE], own[PIECE:], turn[2 * group, 0], turn[2 * group, 1])
                br, bi = times(far[:PIECE], far[PIECE:], turn[2 * group + 1, 0], turn[2 * group + 1, 1])
                image[stage, 1 - now, group, 0] = (ar + br).astype(BF16)
                image[stage, 1 - now, group, 1] = (ai + bi).astype(BF16)

            @pl.when(level == LEVELS - 1)
            def _():
                for group in groups[:-1]:
                    tile_copy(stage, group, sub, group).start()

            return carry

        lax.fori_loop(0, LEVELS, merge, 0)
        own_tile(stage).start()

    for stage in range(STAGES):

        def finish(k, carry):
            peer = lax.rem(sub + k, SUBS)
            tile_copy(stage, peer, peer, peer).wait_recv()
            tile_copy(stage, peer, sub, peer).wait_send()
            image_copy(stage, peer, sub, peer).wait_send()
            return carry

        lax.fori_loop(1, SUBS, finish, 0)
        own_tile(stage).wait()

        def pulses_gone(k, carry):
            peer = lax.rem(rng + k, RANKS)
            pulse_copy(stage, peer, rng, peer).wait_send()
            return carry

        lax.fori_loop(1, RANKS, pulses_gone, 0)
    for k in range(1, SUBS):
        param_copy(sub, lax.rem(sub + k, SUBS)).wait_send()


def tile_kernel(x_hbm, out_hbm, x_ref, out_ref, in_sem, out_sem):
    def read(part, stage):
        lanes = slice(part * RADIX_B, (part + 1) * RADIX_B)
        return pltpu.make_async_copy(
            x_hbm.at[stage, :, :, :, lanes], x_ref.at[part, stage], in_sem.at[part, stage]
        )

    def write(n):
        angles = pl.ds(n * TILE_ANGLES, TILE_ANGLES)
        return pltpu.make_async_copy(out_ref.at[angles], out_hbm.at[angles], out_sem.at[n])

    parts = ANGLES // RADIX_B
    for part in range(parts):
        for stage in range(STAGES):
            read(part, stage).start()
    for part in range(parts):
        for piece in range(RADIX_B // TILE_ANGLES):
            lanes = slice(piece * TILE_ANGLES, (piece + 1) * TILE_ANGLES)
            n = part * (RADIX_B // TILE_ANGLES) + piece
            for stage in range(STAGES):
                if piece == 0:
                    read(part, stage).wait()
                for c in range(2):
                    image = x_ref[part, stage, :, c].reshape(STAGE_BINS, RADIX_B)
                    for row in range(STAGE_ROWS):
                        start = stage * STAGE_BINS + row * RADIX_B
                        values = image[row * RADIX_B : (row + 1) * RADIX_B].T[lanes]
                        out_ref[n * TILE_ANGLES : (n + 1) * TILE_ANGLES, c, start : start + RADIX_B] = values.astype(F32)
            write(n).start()
    for n in range(ANGLES // TILE_ANGLES):
        write(n).wait()


def local(echoes, filter_spectrum, range_shifts, steering, tap_offsets, tap_weights, phase_rates):
    rows = echoes.reshape(PULSES, 2, RADIX_A, RADIX_B).transpose(0, 2, 1, 3).reshape(-1, RADIX_B)
    filt = filter_spectrum.reshape(2, RADIX_A, RADIX_B).transpose(1, 0, 2).reshape(-1, RADIX_B)
    consts = [jnp.asarray(t) for t in tables()]
    operands = [
        range_shifts,
        rows,
        filt,
        steering.reshape(2, ANGLES, PSUB),
        tap_offsets.reshape(2, ANGLES),
        tap_weights.reshape(2, TAPS, ANGLES),
        phase_rates.reshape(2, ANGLES),
        *consts,
    ]
    hbm = pl.BlockSpec(memory_space=pltpu.HBM)
    dma = pltpu.SemaphoreType.DMA
    landing = [
        pltpu.SMEM((PSUB,), jnp.int32),
        pltpu.VMEM((rows.shape[0] + SPARE, RADIX_B), F32),
        pltpu.VMEM((filt.shape[0] + SPARE, RADIX_B), F32),
    ] + [pltpu.VMEM(x.shape, x.dtype) for x in operands[3:]]
    merged = pl.pallas_call(
        kernel,
        out_shape=jax.ShapeDtypeStruct((STAGES, SUBS, 2, PIECE, ANGLES), BF16),
        in_specs=[hbm] * len(operands),
        out_specs=hbm,
        scratch_shapes=[
            *landing,
            pltpu.VMEM((2, RADIX_A, RADIX_B), F32),
            pltpu.VMEM((2 * RADIX_A * PULSES + SPARE, RADIX_B), F32),
            pltpu.VMEM((STAGES, RANKS, 2, STAGE_ROWS, PULSES, RADIX_B), BF16),
            pltpu.VMEM((STAGES, RANKS, 2, STAGE_ROWS, PULSES, RADIX_B), BF16),
            pltpu.VMEM((SUBS, PARAMS, ANGLES), F32),
            pltpu.VMEM((2 * SUBS, ANGLES), F32),
            pltpu.VMEM((6, 2, 2 * SUBS, ANGLES), F32),
            pltpu.VMEM((STAGES, STAGE_BINS, 2 * PSUB), BF16),
            pltpu.VMEM((2 * PSUB, 2 * ANGLES), BF16),
            pltpu.VMEM((2 * SUBS, 2, 2 * RADIX_B, 2 * RADIX_B), BF16),
            pltpu.VMEM((STAGES * LEVELS, 2 * SUBS, 2, PIECE, ANGLES), F32),
            pltpu.VMEM((STAGES, SUBS, 2, PIECE, ANGLES), BF16),
            pltpu.VMEM((STAGES, 2, SUBS, 2, PIECE, ANGLES), BF16),
            dma((len(operands),)), dma((ECHO_PARTS,)), dma((STAGES, RANKS)), dma((STAGES, RANKS)), dma((SUBS,)), dma((SUBS,)),
            dma((STAGES, SUBS)), dma((STAGES, SUBS)), dma((STAGES, SUBS)), dma((STAGES, SUBS)), dma((3 * STAGES,)),
        ],
        compiler_params=pltpu.CompilerParams(
            collective_id=0, has_side_effects=True, vmem_limit_bytes=56 << 20
        ),
        name="merge",
    )(*operands)
    return pl.pallas_call(
        tile_kernel,
        out_shape=jax.ShapeDtypeStruct((ANGLES, 2, BLOCK), F32),
        in_specs=[hbm],
        out_specs=hbm,
        scratch_shapes=[
            pltpu.VMEM((ANGLES // RADIX_B, STAGES, SUBS, 2, PIECE, RADIX_B), BF16),
            pltpu.VMEM((ANGLES, 2, BLOCK), F32),
            dma((ANGLES // RADIX_B, STAGES)),
            dma((ANGLES // TILE_ANGLES,)),
        ],
        compiler_params=pltpu.CompilerParams(vmem_limit_bytes=56 << 20),
        name="tile",
    )(merged)


def solution(mesh):
    placed = (
        P(("sub", "rng"), None, None),
        P(),
        P("sub"),
        P("sub", None, None, None),
        P("sub", None, None),
        P("sub", None, None, None),
        P("sub", None, None),
    )
    return jax.shard_map(
        local, mesh=mesh, in_specs=placed, out_specs=P("sub", None, "rng"), check_vma=False
    )
```

```python
import math

import jax
import jax.numpy as jnp
import ml_dtypes
import numpy as np
from jax import lax
from jax.experimental import pallas as pl
from jax.experimental.pallas import tpu as pltpu
from jax.sharding import PartitionSpec as P

RADIX_A = 96
RADIX_B = 128
ANGLES = 384
TAPS = 4
SAMPLES = 12288
SUBS = 8
RANKS = 16
PULSES = 16
PSUB = RANKS * PULSES
BLOCK = SAMPLES // RANKS
ROWS = BLOCK // RADIX_B
STAGES = 2
STAGE_ROWS = ROWS // STAGES
STAGE_BINS = BLOCK // STAGES
PIECE = STAGE_BINS // SUBS
ECHO_PARTS = 8
HALO = 16
LEVELS = 3
PARAMS = 16
SPARE = 16
IMAGE_ORDER = ((0, 1), (1, 0), (0, 3), (1, 2), (0, 2), (1, 1), (1, 3))
TILE_ORDER = ((0, 1), (1, 0), (0, 3), (1, 2), (0, 2), (1, 1), (1, 3))
TILE_ANGLES = 64
MESH = pl.DeviceIdType.MESH
F32 = jnp.float32
BF16 = jnp.bfloat16


def halves(table, axis):
    high = table.astype(np.float32).astype(ml_dtypes.bfloat16)
    low = (table - high.astype(np.float64)).astype(np.float32).astype(ml_dtypes.bfloat16)
    return np.concatenate([high, high, low], axis=axis)


def tables():
    a = np.arange(RADIX_A)
    b = np.arange(RADIX_B)
    wa = np.exp(-2j * np.pi / RADIX_A * (np.outer(a, a) % RADIX_A))
    wb = np.exp(-2j * np.pi / RADIX_B * (np.outer(b, b) % RADIX_B))
    order = 4 * (b % 32) + b // 32
    wb = wb[:, order]
    vb = np.conj(wb.T)
    va = np.conj(wa)
    left = lambda w: halves(np.block([[w.real, -w.imag], [w.imag, w.real]]), 1)
    right = lambda w: halves(np.block([[w.real, w.imag], [-w.imag, w.real]]), 0)
    turn = np.exp(-2j * np.pi / SAMPLES * np.outer(a, b))
    shifts = np.arange(-HALO, HALO + 1)
    back = np.exp(2j * np.pi / SAMPLES * a[None, :, None] * (b[None, None, :] + shifts[:, None, None])) / SAMPLES
    columns = np.exp(2j * np.pi / RADIX_B * (np.outer(shifts, order) % RADIX_B))
    lanes = np.zeros((2 * HALO + 1, 8, RADIX_B))
    lanes[:, 0], lanes[:, 1] = columns.real, columns.imag
    return (
        left(wa),
        right(wb),
        right(vb),
        left(va),
        np.stack([turn.real, turn.imag]).astype(np.float32),
        np.stack([back.real, back.imag], axis=1).astype(np.float32),
        lanes.astype(np.float32),
    )


def split(x):
    high = x.astype(BF16)
    return high, (x - high.astype(F32)).astype(BF16)


def dot(left, right):
    return jnp.dot(left, right, preferred_element_type=F32)


def left_product(table, x):
    high, low = split(x)
    return dot(table, jnp.concatenate([high, low, high], axis=0))


def right_product(x, table):
    high, low = split(x)
    return dot(jnp.concatenate([high, low, high], axis=1), table)


def times(ar, ai, br, bi):
    return ar * br - ai * bi, ar * bi + ai * br


def load_filter(f_ref, filt):
    lane32 = lax.broadcasted_iota(jnp.int32, (32, RADIX_B), 1)
    for c in range(2):
        f0, f1, f2 = (f_ref[pl.ds(2 * e + c, 32, stride=6), :] for e in range(3))
        parts = [
            f0,
            jnp.where(lane32 < 32, pltpu.roll(f0, 32, 1), pltpu.roll(f1, 32, 1)),
            jnp.where(lane32 < 64, pltpu.roll(f1, 64, 1), pltpu.roll(f2, 64, 1)),
            pltpu.roll(f2, 96, 1),
        ]
        filt[c] = jnp.concatenate(parts, axis=0).T[:RADIX_A]


def compress(first, arrived, shift_ref, x_ref, f_ref, filt, wa, wb, vb, va, tw, back, lanes, rows):
    pairs = range(PULSES // 2)
    pulse = [[2 * j + q for q in range(2)] for j in pairs]
    results = []
    arrived("wa")
    arrived("tw")
    for j in pairs:
        arrived(j)
        signal = []
        for q in range(2):
            start = pulse[j][q] * 2 * RADIX_A
            halves = [x_ref[pl.ds(start + c, RADIX_A, stride=2), :] for c in range(2)]
            signal.append(jnp.concatenate(halves, axis=0))
        results.append(left_product(wa[...], jnp.concatenate(signal, axis=1)))
    arrived("wb")
    for j in pairs:
        turned = []
        for q in range(2):
            part = results[j][:, q * RADIX_B : (q + 1) * RADIX_B]
            turned.append(jnp.concatenate(times(part[:RADIX_A], part[RADIX_A:], tw[0], tw[1]), axis=1))
        results[j] = right_product(jnp.concatenate(turned, axis=0), wb[...])
    arrived("filter")
    arrived("shift")
    arrived("lanes")
    arrived("vb")
    load_filter(f_ref, filt)
    shift = [[shift_ref[first + p] for p in two] for two in pulse]
    for j in pairs:
        turned = []
        for q in range(2):
            part = results[j][q * RADIX_A : (q + 1) * RADIX_A]
            at = shift[j][q] + HALO
            gain = times(filt[0], filt[1], lanes[at, 0:1, :], lanes[at, 1:2, :])
            turned.append(jnp.concatenate(times(part[:, :RADIX_B], part[:, RADIX_B:], *gain), axis=1))
        results[j] = right_product(jnp.concatenate(turned, axis=0), vb[...])
    arrived("back")
    arrived("va")
    for j in pairs:
        turned = []
        for q in range(2):
            part = results[j][q * RADIX_A : (q + 1) * RADIX_A]
            at = shift[j][q] + HALO
            values = times(part[:, :RADIX_B], part[:, RADIX_B:], back[at, 0], back[at, 1])
            turned.append(jnp.concatenate(values, axis=0))
        results[j] = left_product(va[...], jnp.concatenate(turned, axis=1))
    bin8 = lax.broadcasted_iota(jnp.int32, (8, RADIX_B), 0) * RADIX_B
    bin8 = bin8 + lax.broadcasted_iota(jnp.int32, (8, RADIX_B), 1)
    for j in pairs:
        for q in range(2):
            s = shift[j][q]
            for c in range(2):
                values = results[j][c * RADIX_A : (c + 1) * RADIX_A, q * RADIX_B : (q + 1) * RADIX_B]
                top = jnp.where(bin8 + s >= 0, values[:8], 0.0)
                end = jnp.where(bin8 + s < 8 * RADIX_B, values[RADIX_A - 8 :], 0.0)
                values = jnp.concatenate([top, values[8 : RADIX_A - 8], end], axis=0)
                start = c * RADIX_A * PULSES + pulse[j][q]
                rows[pl.ds(start, RADIX_A, stride=PULSES), :] = values


def nth_peer(index, size, k):
    half = size // 2
    across = (size - k) // half
    step = lax.rem(k - across, half)
    return lax.rem(index // half + across, 2) * half + lax.rem(lax.rem(index, half) + step, half)


def kernel(
    shift_hbm, x_hbm, f_hbm, steer_hbm, off_hbm, weight_hbm, rate_hbm,
    wa_hbm, wb_hbm, vb_hbm, va_hbm, tw_hbm, back_hbm, lanes_hbm, out_ref,
    shift_ref, x_ref, f_ref, steer_ref, off_ref, weight_ref, rate_ref, wa, wb, vb, va, tw, back, lanes,
    filt, rows, pulses, held, params, rates, turns, left, steer, band, phase, sent, image,
    load_sem, echo_sem, pulse_send, pulse_recv, param_send, param_recv, image_send, image_recv, tile_send, tile_recv,
    local_sem,
):
    sub = lax.axis_index("sub")
    rng = lax.axis_index("rng")
    barrier = pltpu.get_barrier_semaphore()
    for k in range(1, RANKS):
        pl.semaphore_signal(barrier, inc=1, device_id={"rng": lax.rem(rng + k, RANKS)}, device_id_type=MESH)
    for k in range(1, SUBS):
        pl.semaphore_signal(barrier, inc=1, device_id={"sub": lax.rem(sub + k, SUBS)}, device_id_type=MESH)

    echo_rows = x_hbm.shape[0] // ECHO_PARTS

    def echo_copy(i):
        part = pl.ds(i * echo_rows, echo_rows)
        return pltpu.make_async_copy(x_hbm.at[part], x_ref.at[part], echo_sem.at[i])

    def load(n, src, dst):
        return pltpu.make_async_copy(src, dst, load_sem.at[n])

    names = ["wa", "tw", "wb", "filter", "shift", "lanes", "vb", "va", "back"]
    arrays = [
        (wa_hbm, wa), (tw_hbm, tw), (wb_hbm, wb), (f_hbm, f_ref.at[pl.ds(0, 2 * RADIX_A)]), (shift_hbm, shift_ref), (lanes_hbm, lanes),
        (vb_hbm, vb), (va_hbm, va), (back_hbm, back), (steer_hbm, steer_ref), (off_hbm, off_ref),
        (weight_hbm, weight_ref), (rate_hbm, rate_ref),
    ]
    copies = [load(n, src, dst) for n, (src, dst) in enumerate(arrays)]
    late_loads = copies[len(names) :]
    loads = dict(zip(names, copies))
    loads.update({i: echo_copy(i) for i in range(ECHO_PARTS)})
    order = [0, "wa", 1, "tw", 2, 3, "wb", 4, 5, 6, 7, "filter", "shift", "lanes", "vb", "va", "back"]
    for name in order:
        loads[name].start()
    for copy in late_loads:
        copy.start()

    def arrived(name):
        loads[name].wait()

    compress(rng * PULSES, arrived, shift_ref, x_ref, f_ref, filt, wa, wb, vb, va, tw, back, lanes, rows)

    def pack(j, carry):
        for stage in range(STAGES):
            for c in range(2):
                start = (c * RADIX_A + j * ROWS + stage * STAGE_ROWS) * PULSES
                block = rows[pl.ds(pl.multiple_of(start, PULSES), STAGE_ROWS * PULSES), :].astype(BF16)
                pulses[stage, j, c] = block.reshape(STAGE_ROWS, PULSES, RADIX_B)
        return carry

    lax.fori_loop(0, RANKS, pack, 0)

    pl.semaphore_wait(barrier, RANKS + SUBS - 2)

    def pulse_copy(stage, src, dst, peer):
        return pltpu.make_async_remote_copy(
            src_ref=pulses.at[stage, src], dst_ref=held.at[stage, dst], send_sem=pulse_send.at[stage, src],
            recv_sem=pulse_recv.at[stage, dst], device_id={"rng": peer}, device_id_type=MESH,
        )

    def own_pulses(stage):
        return pltpu.make_async_copy(pulses.at[stage, rng], held.at[stage, rng], local_sem.at[stage])

    for copy in late_loads:
        copy.wait()
    for h in range(2):
        params[sub, 8 * h : 8 * h + 1, :] = off_ref[h : h + 1, :].astype(F32)
        params[sub, 8 * h + 1 : 8 * h + 5, :] = weight_ref[h]
        params[sub, 8 * h + 5 : 8 * h + 6, :] = rate_ref[h : h + 1, :]
        params[sub, 8 * h + 6 : 8 * h + 8, :] = jnp.zeros((2, ANGLES), F32)

    def param_copy(slot, peer):
        return pltpu.make_async_remote_copy(
            src_ref=params.at[slot], dst_ref=params.at[slot], send_sem=param_send.at[peer],
            recv_sem=param_recv.at[slot], device_id={"sub": peer}, device_id_type=MESH,
        )

    for k in range(1, SUBS):
        param_copy(sub, lax.rem(sub + k, SUBS)).start()

    for stage in range(STAGES):

        def send_pulses(k, carry):
            peer = nth_peer(rng, RANKS, k)
            pulse_copy(stage, peer, rng, peer).start()
            return carry

        lax.fori_loop(1, RANKS, send_pulses, 0)
        own_pulses(stage).start()

    def clear(which, carry):
        band[which] = jnp.zeros((2, 2 * RADIX_B, 2 * RADIX_B), BF16)
        return carry

    lax.fori_loop(0, 2 * SUBS, clear, 0)

    real = steer_ref[0].astype(F32)
    imag = steer_ref[1].astype(F32)
    steer[:PSUB, :ANGLES] = real.T.astype(BF16)
    steer[:PSUB, ANGLES:] = imag.T.astype(BF16)
    steer[PSUB:, :ANGLES] = (-imag).T.astype(BF16)
    steer[PSUB:, ANGLES:] = real.T.astype(BF16)

    for k in range(1, SUBS):
        peer = lax.rem(sub + k, SUBS)
        param_copy(peer, peer).wait_recv()

    angle = lax.broadcasted_iota(jnp.int32, (1, ANGLES), 1).astype(F32)
    across = lax.broadcasted_iota(jnp.int32, (RADIX_B, RADIX_B), 0).astype(F32)
    row8 = lax.broadcasted_iota(jnp.int32, (8, ANGLES), 0)
    for group in range(SUBS):
        for h in range(2):
            rates[2 * group + h : 2 * group + h + 1, :] = params[group, 8 * h + 5 : 8 * h + 6, :]
    base = (rng * BLOCK + sub * PIECE).astype(F32)
    for n, bins in enumerate([base, 1.0, 2.0, 4.0, 8.0, float(STAGE_BINS)]):
        at = rates[...] * (bins / SAMPLES)
        turns[n, 0] = jnp.cos(at)
        turns[n, 1] = jnp.sin(at)

    def prepare(which, carry):
        group, h = which // 2, lax.rem(which, 2)
        own = params.at[group, pl.ds(pl.multiple_of(8 * h, 8), 8)]
        sources = [jnp.clip(angle + own[0:1, :] + float(t - 1), 0.0, ANGLES - 1.0) for t in range(TAPS)]
        weights = [own[1 + t : 2 + t, :] for t in range(TAPS)]

        lower = angle < float(ANGLES // 2)
        halved = [[jnp.where(lower == (block == 0), w, 0.0) for w in weights] for block in range(2)]

        def fill(block, first, count, part):
            lanes = slice(part * RADIX_B, (part + 1) * RADIX_B)
            here = across[:count] + float(first)
            total = jnp.zeros((count, RADIX_B), F32)
            for t in range(TAPS):
                total = total + jnp.where(here == sources[t][:, lanes], halved[block][t][:, lanes], 0.0)
            row, col = first - block * RADIX_B, (part - block) * RADIX_B
            band[which, block, row : row + count, col : col + RADIX_B] = total.astype(BF16)

        fill(0, 0, 128, 0)
        fill(0, 128, 16, 0)
        fill(0, 112, 16, 1)
        fill(0, 128, 80, 1)
        fill(1, 176, 80, 1)
        fill(1, 256, 16, 1)
        fill(1, 240, 16, 2)
        fill(1, 256, 128, 2)

        def turn(n):
            return tuple(turns[n, c, pl.ds(which, 1), :] for c in range(2))

        def chosen(n, bit):
            real, imag = turn(n)
            on = lax.rem(row8 // bit, 2) == 1
            return jnp.where(on, real, 1.0), jnp.where(on, imag, 0.0)

        start = times(*times(*times(*chosen(1, 1), *chosen(2, 2)), *chosen(3, 4)), *turn(0))
        by8, by_stage = turn(4), turn(5)
        for stage in range(STAGES):
            if stage:
                start = times(*start, *by_stage)
            at = start
            for t in range(PIECE // 8):
                part = slice(8 * t, 8 * t + 8)
                now = at
                for level in range(LEVELS):
                    phase[stage * LEVELS + level, which, 0, part, :] = now[0]
                    phase[stage * LEVELS + level, which, 1, part, :] = now[1]
                    if level < LEVELS - 1:
                        now = times(*now, *at)
                if t < PIECE // 8 - 1:
                    at = times(*at, *by8)
        return carry

    lax.fori_loop(0, 2 * SUBS, prepare, 0)

    def across(flip, step):
        return lax.rem(sub // 4 + flip, 2) * 4 + lax.rem(lax.rem(sub, 4) + step, 4)

    def image_copy(stage, src, dst, peer):
        return pltpu.make_async_remote_copy(
            src_ref=sent.at[stage, src], dst_ref=image.at[stage, 0, dst], send_sem=image_send.at[stage, src],
            recv_sem=image_recv.at[stage, dst], device_id={"sub": peer}, device_id_type=MESH,
        )

    def own_image(stage):
        return pltpu.make_async_copy(sent.at[stage, sub], image.at[stage, 0, sub], local_sem.at[STAGES + stage])

    for stage in range(STAGES):

        def pulses_here(k, carry):
            peer = lax.rem(rng + k, RANKS)
            pulse_copy(stage, peer, peer, peer).wait_recv()
            return carry

        lax.fori_loop(1, RANKS, pulses_here, 0)
        own_pulses(stage).wait()
        for row in range(STAGE_ROWS):
            for c in range(2):
                block = held[stage, :, c, row].reshape(PSUB, RADIX_B)
                left[stage, row * RADIX_B : (row + 1) * RADIX_B, c * PSUB : (c + 1) * PSUB] = block.T

        parts = dot(left[stage], steer[...]).astype(BF16)
        for c in range(2):
            sent[stage, :, c] = parts[:, c * ANGLES : (c + 1) * ANGLES].reshape(SUBS, PIECE, ANGLES)

        for flip, step in IMAGE_ORDER:
            peer = across(flip, step)
            image_copy(stage, peer, sub, peer).start()
        own_image(stage).start()

    def resampled(values, which):
        values = values.reshape(2 * PIECE, ANGLES)
        low = dot(values[:, : 2 * RADIX_B], band[which, 0])
        high = dot(values[:, RADIX_B:], band[which, 1])
        middle = low[:, RADIX_B:] + high[:, :RADIX_B]
        return jnp.concatenate([low[:, :RADIX_B], middle, high[:, RADIX_B:]], axis=1)

    def tile_copy(stage, src, dst, peer):
        return pltpu.make_async_remote_copy(
            src_ref=image.at[stage, 1, src], dst_ref=out_ref.at[stage, dst], send_sem=tile_send.at[stage, src],
            recv_sem=tile_recv.at[stage, dst], device_id={"sub": peer}, device_id_type=MESH,
        )

    def own_tile(stage):
        return pltpu.make_async_copy(
            image.at[stage, 1, sub], out_ref.at[stage, sub], local_sem.at[2 * STAGES + stage]
        )

    for stage in range(STAGES):

        def image_here(k, carry):
            peer = lax.rem(sub + k, SUBS)
            image_copy(stage, peer, peer, peer).wait_recv()
            return carry

        lax.fori_loop(1, SUBS, image_here, 0)
        own_image(stage).wait()

        def merge(i, carry):
            level = i
            now = lax.rem(level, 2)
            bit = 1 + level + level // 2
            turn = phase.at[stage * LEVELS + level]
            groups = [across(flip, step) for flip, step in TILE_ORDER] + [sub]
            pairs = []
            for group in groups:
                far_group = group + bit - 2 * bit * lax.rem(group // bit, 2)
                own = resampled(image[stage, now, group], 2 * group)
                far = resampled(image[stage, now, far_group], 2 * group + 1)
                pairs.append((own, far))
            for group, (own, far) in zip(groups, pairs):
                ar, ai = times(own[:PIECE], own[PIECE:], turn[2 * group, 0], turn[2 * group, 1])
                br, bi = times(far[:PIECE], far[PIECE:], turn[2 * group + 1, 0], turn[2 * group + 1, 1])
                image[stage, 1 - now, group, 0] = (ar + br).astype(BF16)
                image[stage, 1 - now, group, 1] = (ai + bi).astype(BF16)

            @pl.when(level == LEVELS - 1)
            def _():
                for group in groups[:-1]:
                    tile_copy(stage, group, sub, group).start()

            return carry

        lax.fori_loop(0, LEVELS, merge, 0)
        own_tile(stage).start()

    for stage in range(STAGES):

        def finish(k, carry):
            peer = lax.rem(sub + k, SUBS)
            tile_copy(stage, peer, peer, peer).wait_recv()
            tile_copy(stage, peer, sub, peer).wait_send()
            image_copy(stage, peer, sub, peer).wait_send()
            return carry

        lax.fori_loop(1, SUBS, finish, 0)
        own_tile(stage).wait()

        def pulses_gone(k, carry):
            peer = lax.rem(rng + k, RANKS)
            pulse_copy(stage, peer, rng, peer).wait_send()
            return carry

        lax.fori_loop(1, RANKS, pulses_gone, 0)
    for k in range(1, SUBS):
        param_copy(sub, lax.rem(sub + k, SUBS)).wait_send()


def tile_kernel(x_hbm, out_hbm, x_ref, out_ref, in_sem, out_sem):
    def read(part, stage):
        lanes = slice(part * RADIX_B, (part + 1) * RADIX_B)
        return pltpu.make_async_copy(
            x_hbm.at[stage, :, :, :, lanes], x_ref.at[part, stage], in_sem.at[part, stage]
        )

    def write(n):
        angles = pl.ds(n * TILE_ANGLES, TILE_ANGLES)
        return pltpu.make_async_copy(out_ref.at[angles], out_hbm.at[angles], out_sem.at[n])

    parts = ANGLES // RADIX_B
    for part in range(parts):
        for stage in range(STAGES):
            read(part, stage).start()
    for part in range(parts):
        for piece in range(RADIX_B // TILE_ANGLES):
            lanes = slice(piece * TILE_ANGLES, (piece + 1) * TILE_ANGLES)
            n = part * (RADIX_B // TILE_ANGLES) + piece
            for stage in range(STAGES):
                if piece == 0:
                    read(part, stage).wait()
                for c in range(2):
                    image = x_ref[part, stage, :, c].reshape(STAGE_BINS, RADIX_B)
                    for row in range(STAGE_ROWS):
                        start = stage * STAGE_BINS + row * RADIX_B
                        values = image[row * RADIX_B : (row + 1) * RADIX_B].T[lanes]
                        out_ref[n * TILE_ANGLES : (n + 1) * TILE_ANGLES, c, start : start + RADIX_B] = values.astype(F32)
            write(n).start()
    for n in range(ANGLES // TILE_ANGLES):
        write(n).wait()


def local(echoes, filter_spectrum, range_shifts, steering, tap_offsets, tap_weights, phase_rates):
    rows = echoes.reshape(PULSES, 2, RADIX_A, RADIX_B).transpose(0, 2, 1, 3).reshape(-1, RADIX_B)
    filt = filter_spectrum.reshape(2, RADIX_A, RADIX_B).transpose(1, 0, 2).reshape(-1, RADIX_B)
    consts = [jnp.asarray(t) for t in tables()]
    operands = [
        range_shifts,
        rows,
        filt,
        steering.reshape(2, ANGLES, PSUB),
        tap_offsets.reshape(2, ANGLES),
        tap_weights.reshape(2, TAPS, ANGLES),
        phase_rates.reshape(2, ANGLES),
        *consts,
    ]
    hbm = pl.BlockSpec(memory_space=pltpu.HBM)
    dma = pltpu.SemaphoreType.DMA
    landing = [
        pltpu.SMEM((PSUB,), jnp.int32),
        pltpu.VMEM((rows.shape[0] + SPARE, RADIX_B), F32),
        pltpu.VMEM((filt.shape[0] + SPARE, RADIX_B), F32),
    ] + [pltpu.VMEM(x.shape, x.dtype) for x in operands[3:]]
    merged = pl.pallas_call(
        kernel,
        out_shape=jax.ShapeDtypeStruct((STAGES, SUBS, 2, PIECE, ANGLES), BF16),
        in_specs=[hbm] * len(operands),
        out_specs=hbm,
        scratch_shapes=[
            *landing,
            pltpu.VMEM((2, RADIX_A, RADIX_B), F32),
            pltpu.VMEM((2 * RADIX_A * PULSES + SPARE, RADIX_B), F32),
            pltpu.VMEM((STAGES, RANKS, 2, STAGE_ROWS, PULSES, RADIX_B), BF16),
            pltpu.VMEM((STAGES, RANKS, 2, STAGE_ROWS, PULSES, RADIX_B), BF16),
            pltpu.VMEM((SUBS, PARAMS, ANGLES), F32),
            pltpu.VMEM((2 * SUBS, ANGLES), F32),
            pltpu.VMEM((6, 2, 2 * SUBS, ANGLES), F32),
            pltpu.VMEM((STAGES, STAGE_BINS, 2 * PSUB), BF16),
            pltpu.VMEM((2 * PSUB, 2 * ANGLES), BF16),
            pltpu.VMEM((2 * SUBS, 2, 2 * RADIX_B, 2 * RADIX_B), BF16),
            pltpu.VMEM((STAGES * LEVELS, 2 * SUBS, 2, PIECE, ANGLES), F32),
            pltpu.VMEM((STAGES, SUBS, 2, PIECE, ANGLES), BF16),
            pltpu.VMEM((STAGES, 2, SUBS, 2, PIECE, ANGLES), BF16),
            dma((len(operands),)), dma((ECHO_PARTS,)), dma((STAGES, RANKS)), dma((STAGES, RANKS)), dma((SUBS,)), dma((SUBS,)),
            dma((STAGES, SUBS)), dma((STAGES, SUBS)), dma((STAGES, SUBS)), dma((STAGES, SUBS)), dma((3 * STAGES,)),
        ],
        compiler_params=pltpu.CompilerParams(
            collective_id=0, has_side_effects=True, vmem_limit_bytes=56 << 20
        ),
        name="merge",
    )(*operands)
    return pl.pallas_call(
        tile_kernel,
        out_shape=jax.ShapeDtypeStruct((ANGLES, 2, BLOCK), F32),
        in_specs=[hbm],
        out_specs=hbm,
        scratch_shapes=[
            pltpu.VMEM((ANGLES // RADIX_B, STAGES, SUBS, 2, PIECE, RADIX_B), BF16),
            pltpu.VMEM((ANGLES, 2, BLOCK), F32),
            dma((ANGLES // RADIX_B, STAGES)),
            dma((ANGLES // TILE_ANGLES,)),
        ],
        compiler_params=pltpu.CompilerParams(vmem_limit_bytes=56 << 20),
        name="tile",
    )(merged)


def solution(mesh):
    placed = (
        P(("sub", "rng"), None, None),
        P(),
        P("sub"),
        P("sub", None, None, None),
        P("sub", None, None),
        P("sub", None, None, None),
        P("sub", None, None),
    )
    return jax.shard_map(
        local, mesh=mesh, in_specs=placed, out_specs=P("sub", None, "rng"), check_vma=False
    )
```
